128 devices in a mesh: tm: 8 (over y_lo, z), space: 16 (over y_hi, x, core).
Axes of the slice: x: 4, y: 4 (y_hi: 2, y_lo: 2; y = y_hi * 2 + y_lo), z: 4, core: 2. Of those that a mesh axis runs over, the one named last changes fastest.
Arguments:
- snapshots: bfloat16 [1024, 786432], P('tm', 'space'), may hold values from -10 to 10, as said below
- area_weight: float32 [786432], P('space'), may hold values from 0.1 to 1
- eigvecs: bfloat16 [1024, 64], replicated, may hold values from -0.1875 to 0.1875
- eigvals: float32 [64], replicated, may hold values from 0.5 to 8
Outputs:
- gram: float32 [1024, 1024], P(('tm', 'space'))
- modes: bfloat16 [64, 786432], P('tm', 'space')
The draws below stay inside these ranges and needn't reach their ends.
Inputs may be any that keep to these rules, and one draw needn't show every extreme that they name: `snapshots`: a per-column climatology plus hourly departures.
All inputs are finite; a program needn't handle non-finite values.
Results may differ from the reference program's by a relative error of at most 0.01.
Values may be sent and summed in bfloat16 or wider, within the bound.
A program may use at most 128 MiB of HBM per device.

```python
import math
import jax
import jax.numpy as jnp
from jax import lax

CELL_DEV = 49152
MODES = 64
TIME = 1024
CELLS = 786432


def draw_snapshots(key, part):
    first = jax.random.fold_in(key, 11)
    second = jax.random.fold_in(key, 12)
    climate = jax.random.uniform(first, (1, CELLS), jnp.float32, -2.0, 2.0)
    noise = jax.random.normal(second, (TIME, CELLS), jnp.float32)
    noise = jnp.clip(noise, -8.0, 8.0)
    return (climate + noise).astype(jnp.bfloat16)


def level_of(own_key, dims, split, low, top_value):
    factor_of, own = 1.0, jax.random.fold_in(own_key, 6)
    for dim, parts in split:
        steps = jnp.exp(jax.random.uniform(jax.random.fold_in(own, dim), (parts,), jnp.float32, low / len(split), top_value / len(split)))
        factor_of = factor_of * jnp.repeat(steps, dims[dim] // parts).reshape([-1 if axis == dim else 1 for axis in range(len(dims))])
    return factor_of


def centred(own_key, dims, deviation, reach, kind=jnp.bfloat16):
    return jnp.clip(deviation * jax.random.normal(own_key, dims, jnp.float32), -reach, reach).astype(kind)


def setup_inputs(seed: int = 0) -> dict:
    splits = jax.random.split(jax.random.key(seed), 5)
    return {
        "snapshots": draw_snapshots(jax.random.fold_in(splits[4], 71), 0),
        "area_weight": jnp.clip(jnp.exp(math.log(1.0) - 2.3025851 * jax.random.uniform(splits[1], (CELLS,), jnp.float32) ** level_of(splits[1], (CELLS,), ((0, 16),), -0.2, 0.2)), 0.1, 1.0),
        "eigvecs": centred(splits[2], (TIME, MODES), TIME ** -0.5, 0.1875),
        "eigvals": jnp.clip(jnp.exp(jax.random.uniform(splits[3], (MODES,), jnp.float32, math.log(0.5), math.log(8.0))), 0.5, 8.0),
    }


def reference(snapshots, area_weight, eigvecs, eigvals):
    width = CELL_DEV
    count = CELLS // width
    inv_root = 1.0 / jnp.sqrt(eigvals)

    def step(total, index):
        start = (index * width).astype(jnp.int32)
        block = lax.dynamic_slice_in_dim(snapshots, start, width, 1).astype(jnp.float32)
        weight = lax.dynamic_slice_in_dim(area_weight, start, width, 0)
        mean = lax.optimization_barrier(jnp.sum(block, axis=0)) / TIME
        weighted = (jnp.sqrt(weight)[None, :] * (block - mean[None, :])).astype(jnp.bfloat16)
        part = lax.dot_general(weighted, weighted, (((1,), (1,)), ((), ())), preferred_element_type=jnp.float32)
        proj = jnp.dot(eigvecs.T, weighted, preferred_element_type=jnp.float32)
        mode_block = (proj * inv_root[:, None]).astype(jnp.bfloat16)
        return (total + part, mode_block)
    init = jnp.zeros((TIME, TIME), jnp.float32)
    total, mode_blocks = lax.scan(step, init, jnp.arange(count, dtype=jnp.int32))
    modes = jnp.transpose(mode_blocks, (1, 0, 2)).reshape(MODES, CELLS)
    return (total / CELLS, modes)
```

```python
import functools

import jax
import jax.numpy as jnp
from jax import lax
from jax.experimental import pallas as pl
from jax.experimental.pallas import tpu as pltpu
from jax.sharding import PartitionSpec as P

MESH = pl.DeviceIdType.MESH
CHUNKS = 8
AHEAD = 3


def kernel(snap, area, evt, evals, gram_out, modes_out,
           buf, wbuf, acc, inv, area_v, msend, csend, crecv, xsend, xrecv, part, ysend, yrecv,
           s_send, s_recv, s_own, s_area, m_send, m_recv, m_own,
           c_send, c_recv, x_send, x_recv, y_send, y_recv):
    time_dev, cell_dev = snap.shape
    times, sub = buf.shape
    width = wbuf.shape[1]
    modes_n = evt.shape[0]
    cells = cell_dev * 16
    half = times // 2

    tm = lax.axis_index("tm")
    sp = lax.axis_index("space")
    y_lo, z = tm // 4, lax.rem(tm, 4)
    y_hi, x, core = sp // 8, lax.rem(sp // 2, 4), lax.rem(sp, 2)

    def tm_of(j, sign):
        return lax.rem(y_lo + j // 4, 2) * 4 + lax.rem(z + sign * (j % 4) + 4, 4)

    def sp_x(dx, sign):
        return y_hi * 8 + lax.rem(x + sign * dx + 4, 4) * 2 + core

    def yz_of(j, sign):
        return tm_of(j % 8, sign), lax.rem(y_hi + j // 8, 2)

    def yz_dev(j, sign):
        t, h = yz_of(j, sign)
        return (t, h * 8 + x * 2 + core)

    other = (tm, sp + 1 - 2 * core)

    barrier = pltpu.get_barrier_semaphore()
    partners = [yz_dev(j, 1) for j in range(1, 16)] + [other] + [(tm, sp_x(d, 1)) for d in (1, 2, 3)]
    for device in partners:
        pl.semaphore_signal(barrier, inc=1, device_id=device, device_id_type=MESH)
    pl.semaphore_wait(barrier, len(partners))

    def raw(k, j, sign):
        peer = tm_of(j, sign)
        cols = pl.ds(pl.multiple_of(k * width, 128), width)
        row = tm if sign > 0 else peer
        return pltpu.make_async_remote_copy(
            src_ref=snap.at[:, pl.ds(pl.multiple_of(peer * sub + k * width, 128), width)],
            dst_ref=buf.at[pl.ds(pl.multiple_of(row * time_dev, 128), time_dev), cols],
            send_sem=s_send.at[k, j - 1], recv_sem=s_recv.at[k, j - 1],
            device_id=(peer, sp), device_id_type=MESH)

    own_copy = pltpu.make_async_copy(
        snap.at[:, pl.ds(pl.multiple_of(tm * sub, 128), sub)],
        buf.at[pl.ds(pl.multiple_of(tm * time_dev, 128), time_dev), :], s_own)
    area_rows = sub // 128
    area_copy = pltpu.make_async_copy(
        area.at[pl.ds(pl.multiple_of(tm * area_rows, 8), area_rows), :], area_v, s_area)

    def start_chunk(k):
        for j in range(1, 8):
            raw(k, j, 1).start()

    for k in range(AHEAD):
        start_chunk(k)
    own_copy.start()
    area_copy.start()

    acc[...] = jnp.zeros_like(acc)
    eye = lax.broadcasted_iota(jnp.int32, (modes_n, modes_n), 0) == lax.broadcasted_iota(
        jnp.int32, (modes_n, modes_n), 1)
    inv[...] = 1.0 / jnp.sqrt(jnp.sum(
        jnp.where(eye, jnp.broadcast_to(evals[...], (modes_n, modes_n)), 0.0), axis=1, keepdims=True))
    area_copy.wait()
    area_v[...] = jnp.sqrt(area_v[...])
    own_copy.wait()

    strips = width // 128

    def chunk(k, carry):
        for j in range(1, 8):
            raw(k, j, -1).wait_recv()
        for j in range(1, 8):
            raw(k, j, 1).wait_send()

        @pl.when(k + AHEAD < CHUNKS)
        def _():
            start_chunk(k + AHEAD)

        base = pl.multiple_of(k * width, 128)
        cols = pl.ds(base, width)

        def add(i, total):
            block = buf[pl.ds(pl.multiple_of(i * 64, 64), 64), cols].astype(jnp.float32)
            return total + jnp.sum(block.reshape(8, 8, width), axis=0)

        total = lax.fori_loop(0, times // 64, add, jnp.zeros((8, width), jnp.float32))
        mean = jnp.sum(total, axis=0, keepdims=True) / times
        root = jnp.concatenate(
            [area_v[pl.ds(k * strips + s, 1), :] for s in range(strips)], axis=1)

        def weigh(i, c):
            rows = pl.ds(pl.multiple_of(i * 64, 64), 64)
            block = buf[rows, cols].astype(jnp.float32)
            wbuf[rows, :] = (root * (block - mean)).astype(jnp.bfloat16)
            return c

        lax.fori_loop(0, times // 64, weigh, 0)

        def gram(i, c):
            tile = pl.ds(pl.multiple_of(i * 256, 256), 256)
            acc[:, tile] += lax.dot_general(
                wbuf[...], wbuf[tile, :], (((1,), (1,)), ((), ())),
                preferred_element_type=jnp.float32)
            return c

        lax.fori_loop(0, times // 256, gram, 0)
        proj = jnp.dot(evt[...], wbuf[...], preferred_element_type=jnp.float32) * inv[...]
        proj = proj.astype(jnp.bfloat16)
        for p in range(8):
            msend[p, :, cols] = proj[p * 8:p * 8 + 8, :]
        return carry

    lax.fori_loop(0, CHUNKS, chunk, 0)

    own_cols = pl.ds(pl.multiple_of(tm * sub, 128), sub)

    def modes_copy(j, sign):
        peer = tm_of(j, sign)
        col = tm if sign > 0 else peer
        return pltpu.make_async_remote_copy(
            src_ref=msend.at[peer],
            dst_ref=modes_out.at[:, pl.ds(pl.multiple_of(col * sub, 128), sub)],
            send_sem=m_send.at[j - 1], recv_sem=m_recv.at[j - 1],
            device_id=(peer, sp), device_id_type=MESH)

    for j in range(1, 8):
        modes_copy(j, 1).start()
    modes_own = pltpu.make_async_copy(msend.at[tm], modes_out.at[:, own_cols], m_own)
    modes_own.start()

    def unit(g, dx, which):
        at = ((g * 4 + lax.rem(x + dx, 4)) * 2 + which) * 8
        rows = acc[pl.ds(pl.multiple_of(at, 8), 8), :]
        return jnp.concatenate([rows[:, :half], rows[:, half:]], axis=0)

    def core_copy(dx):
        return pltpu.make_async_remote_copy(
            src_ref=csend.at[dx], dst_ref=crecv.at[dx],
            send_sem=c_send.at[dx], recv_sem=c_recv.at[dx],
            device_id=other, device_id_type=MESH)

    def x_copy(dx, sign):
        return pltpu.make_async_remote_copy(
            src_ref=xsend.at[dx - 1], dst_ref=xrecv.at[dx - 1],
            send_sem=x_send.at[dx - 1], recv_sem=x_recv.at[dx - 1],
            device_id=(tm, sp_x(dx, sign)), device_id_type=MESH)

    order = (2, 1, 3, 0)
    for dx in order:
        def pack(g, c, dx=dx):
            csend[dx, g] = unit(g, dx, 1 - core).astype(jnp.bfloat16)
            return c
        lax.fori_loop(0, 16, pack, 0)
        core_copy(dx).start()

    for dx in order:
        core_copy(dx).wait_recv()

        def merge(g, c, dx=dx):
            value = unit(g, dx, core) + crecv[dx, g].astype(jnp.float32)
            if dx:
                xsend[dx - 1, g] = value.astype(jnp.bfloat16)
            else:
                part[g] = value
            return c
        lax.fori_loop(0, 16, merge, 0)
        if dx:
            x_copy(dx, 1).start()
    for dx in (1, 2, 3):
        x_copy(dx, -1).wait_recv()

    def merge_x(g, c):
        value = part[g]
        for d in range(3):
            value = value + xrecv[d, g].astype(jnp.float32)
        part[g] = value
        ysend[g] = value.astype(jnp.bfloat16)
        return c
    lax.fori_loop(0, 16, merge_x, 0)

    def y_copy(j, sign):
        t, h = yz_of(j, sign)
        return pltpu.make_async_remote_copy(
            src_ref=ysend.at[t * 2 + h], dst_ref=yrecv.at[j - 1],
            send_sem=y_send.at[j - 1], recv_sem=y_recv.at[j - 1],
            device_id=(t, h * 8 + x * 2 + core), device_id_type=MESH)

    for j in range(1, 16):
        y_copy(j, 1).start()
    total = part[tm * 2 + y_hi]
    for j in range(1, 16):
        y_copy(j, -1).wait_recv()
        total = total + yrecv[j - 1].astype(jnp.float32)
    total = total / cells
    gram_out[:, :half] = total[:8, :]
    gram_out[:, half:] = total[8:, :]

    modes_own.wait()
    for j in range(1, 8):
        modes_copy(j, -1).wait_recv()
        modes_copy(j, 1).wait_send()
    for dx in range(4):
        core_copy(dx).wait_send()
    for dx in (1, 2, 3):
        x_copy(dx, 1).wait_send()
    for j in range(1, 16):
        y_copy(j, 1).wait_send()


def local(snapshots, area_weight, eigvecs, eigvals):
    tm_count = lax.axis_size("tm")
    time_dev, cell_dev = snapshots.shape
    times = time_dev * tm_count
    sub = cell_dev // tm_count
    modes_n = eigvecs.shape[1]
    width = sub // CHUNKS
    vmem = pl.BlockSpec(memory_space=pltpu.VMEM)
    hbm = pl.BlockSpec(memory_space=pl.ANY)
    bf16, f32 = jnp.bfloat16, jnp.float32
    half = times // 2
    dma = pltpu.SemaphoreType.DMA
    return pl.pallas_call(
        kernel,
        out_shape=(jax.ShapeDtypeStruct((8, times), f32), jax.ShapeDtypeStruct((8, cell_dev), bf16)),
        in_specs=[hbm, hbm, vmem, vmem],
        out_specs=(vmem, hbm),
        scratch_shapes=[
            pltpu.VMEM((times, sub), bf16),
            pltpu.VMEM((times, width), bf16),
            pltpu.VMEM((times, times), f32),
            pltpu.VMEM((modes_n, 1), f32),
            pltpu.VMEM((sub // 128, 128), f32),
            pltpu.VMEM((tm_count, 8, sub), bf16),
            pltpu.VMEM((4, 16, 16, half), bf16),
            pltpu.VMEM((4, 16, 16, half), bf16),
            pltpu.VMEM((3, 16, 16, half), bf16),
            pltpu.VMEM((3, 16, 16, half), bf16),
            pltpu.VMEM((16, 16, half), f32),
            pltpu.VMEM((16, 16, half), bf16),
            pltpu.VMEM((15, 16, half), bf16),
            dma((CHUNKS, 7)), dma((CHUNKS, 7)), dma, dma,
            dma((7,)), dma((7,)), dma,
            dma((4,)), dma((4,)), dma((3,)), dma((3,)), dma((15,)), dma((15,)),
        ],
        compiler_params=pltpu.CompilerParams(
            collective_id=0, has_side_effects=True, vmem_limit_bytes=48 << 20),
        cost_estimate=pl.CostEstimate(
            flops=2 * times * times * sub, bytes_accessed=2 * times * sub, transcendentals=0),
    )(snapshots, area_weight.reshape(-1, 128), eigvecs.T, eigvals.reshape(1, -1))


def solution(mesh):
    in_specs = (P("tm", "space"), P("space"), P(), P())
    out_specs = (P(("tm", "space"), None), P("tm", "space"))
    return jax.shard_map(local, mesh=mesh, in_specs=in_specs, out_specs=out_specs, check_vma=False)
```

```python
import functools

import jax
import jax.numpy as jnp
from jax import lax
from jax.experimental import pallas as pl
from jax.experimental.pallas import tpu as pltpu
from jax.sharding import PartitionSpec as P

MESH = pl.DeviceIdType.MESH
CHUNKS = 12
AHEAD = 4


def kernel(snap, area, evt_in, evals_in, gram_out, modes_out,
           buf, wbuf, acc, evt, evals, inv, area_v, msend, csend, crecv, xsend, xrecv, part, ysend, yrecv,
           s_send, s_recv, s_own, s_area, s_evt, s_evals, m_send, m_recv, m_own,
           c_send, c_recv, x_send, x_recv, y_send, y_recv):
    time_dev, cell_dev = snap.shape
    times, sub = buf.shape
    width = wbuf.shape[1]
    modes_n = evt.shape[0]
    cells = cell_dev * 16
    half = times // 2

    tm = lax.axis_index("tm")
    sp = lax.axis_index("space")
    y_lo, z = tm // 4, lax.rem(tm, 4)
    y_hi, x, core = sp // 8, lax.rem(sp // 2, 4), lax.rem(sp, 2)

    def tm_of(j, sign):
        return lax.rem(y_lo + j // 4, 2) * 4 + lax.rem(z + sign * (j % 4) + 4, 4)

    def sp_x(dx, sign):
        return y_hi * 8 + lax.rem(x + sign * dx + 4, 4) * 2 + core

    def yz_of(j, sign):
        return tm_of(j % 8, sign), lax.rem(y_hi + j // 8, 2)

    def yz_dev(j, sign):
        t, h = yz_of(j, sign)
        return (t, h * 8 + x * 2 + core)

    other = (tm, sp + 1 - 2 * core)

    barrier = pltpu.get_barrier_semaphore()
    partners = [yz_dev(j, 1) for j in range(1, 16)] + [other] + [(tm, sp_x(d, 1)) for d in (1, 2, 3)]
    for device in partners:
        pl.semaphore_signal(barrier, inc=1, device_id=device, device_id_type=MESH)
    pl.semaphore_wait(barrier, len(partners))

    def raw(k, j, sign):
        peer = tm_of(j, sign)
        cols = pl.ds(pl.multiple_of(k * width, 128), width)
        row = tm if sign > 0 else peer
        return pltpu.make_async_remote_copy(
            src_ref=snap.at[:, pl.ds(pl.multiple_of(peer * sub + k * width, 128), width)],
            dst_ref=buf.at[pl.ds(pl.multiple_of(row * time_dev, 128), time_dev), cols],
            send_sem=s_send.at[k, j - 1], recv_sem=s_recv.at[k, j - 1],
            device_id=(peer, sp), device_id_type=MESH)

    own_copy = pltpu.make_async_copy(
        snap.at[:, pl.ds(pl.multiple_of(tm * sub, 128), sub)],
        buf.at[pl.ds(pl.multiple_of(tm * time_dev, 128), time_dev), :], s_own)
    area_rows = sub // 128
    area_copy = pltpu.make_async_copy(
        area.at[pl.ds(pl.multiple_of(tm * area_rows, 8), area_rows), :], area_v, s_area)

    def start_chunk(k):
        for j in range(1, 8):
            raw(k, j, 1).start()

    for k in range(AHEAD):
        start_chunk(k)
    own_copy.start()
    area_copy.start()
    evt_copy = pltpu.make_async_copy(evt_in, evt, s_evt)
    evals_copy = pltpu.make_async_copy(evals_in, evals, s_evals)
    evals_copy.start()
    evt_copy.start()

    acc[...] = jnp.zeros_like(acc)
    evals_copy.wait()
    evt_copy.wait()
    eye = lax.broadcasted_iota(jnp.int32, (modes_n, modes_n), 0) == lax.broadcasted_iota(
        jnp.int32, (modes_n, modes_n), 1)
    inv[...] = 1.0 / jnp.sqrt(jnp.sum(
        jnp.where(eye, jnp.broadcast_to(evals[...], (modes_n, modes_n)), 0.0), axis=1, keepdims=True))
    area_copy.wait()
    area_v[...] = jnp.sqrt(area_v[...])
    own_copy.wait()

    strips = width // 128

    def chunk(k, carry):
        for j in range(1, 8):
            raw(k, j, -1).wait_recv()
        for j in range(1, 8):
            raw(k, j, 1).wait_send()

        @pl.when(k + AHEAD < CHUNKS)
        def _():
            start_chunk(k + AHEAD)

        base = pl.multiple_of(k * width, 128)
        cols = pl.ds(base, width)

        def add(i, total):
            block = buf[pl.ds(pl.multiple_of(i * 64, 64), 64), cols].astype(jnp.float32)
            return total + jnp.sum(block.reshape(8, 8, width), axis=0)

        total = lax.fori_loop(0, times // 64, add, jnp.zeros((8, width), jnp.float32))
        mean = jnp.sum(total, axis=0, keepdims=True) / times
        root = jnp.concatenate(
            [area_v[pl.ds(k * strips + s, 1), :] for s in range(strips)], axis=1)

        def weigh(i, c):
            rows = pl.ds(pl.multiple_of(i * 64, 64), 64)
            block = buf[rows, cols].astype(jnp.float32)
            wbuf[rows, :] = (root * (block - mean)).astype(jnp.bfloat16)
            return c

        lax.fori_loop(0, times // 64, weigh, 0)

        def gram(i, c):
            tile = pl.ds(pl.multiple_of(i * 256, 256), 256)
            acc[:, tile] += lax.dot_general(
                wbuf[...], wbuf[tile, :], (((1,), (1,)), ((), ())),
                preferred_element_type=jnp.float32)
            return c

        lax.fori_loop(0, times // 256, gram, 0)
        proj = jnp.dot(evt[...], wbuf[...], preferred_element_type=jnp.float32) * inv[...]
        proj = proj.astype(jnp.bfloat16)
        for p in range(8):
            msend[p, :, cols] = proj[p * 8:p * 8 + 8, :]
        return carry

    lax.fori_loop(0, CHUNKS, chunk, 0)

    own_cols = pl.ds(pl.multiple_of(tm * sub, 128), sub)

    def modes_copy(j, sign):
        peer = tm_of(j, sign)
        col = tm if sign > 0 else peer
        return pltpu.make_async_remote_copy(
            src_ref=msend.at[peer],
            dst_ref=modes_out.at[:, pl.ds(pl.multiple_of(col * sub, 128), sub)],
            send_sem=m_send.at[j - 1], recv_sem=m_recv.at[j - 1],
            device_id=(peer, sp), device_id_type=MESH)

    for j in range(1, 8):
        modes_copy(j, 1).start()
    modes_own = pltpu.make_async_copy(msend.at[tm], modes_out.at[:, own_cols], m_own)
    modes_own.start()

    def unit(g, dx, which):
        at = ((g * 4 + lax.rem(x + dx, 4)) * 2 + which) * 8
        rows = acc[pl.ds(pl.multiple_of(at, 8), 8), :]
        return jnp.concatenate([rows[:, :half], rows[:, half:]], axis=0)

    def core_copy(dx):
        return pltpu.make_async_remote_copy(
            src_ref=csend.at[dx], dst_ref=crecv.at[dx],
            send_sem=c_send.at[dx], recv_sem=c_recv.at[dx],
            device_id=other, device_id_type=MESH)

    def x_copy(dx, sign):
        return pltpu.make_async_remote_copy(
            src_ref=xsend.at[dx - 1], dst_ref=xrecv.at[dx - 1],
            send_sem=x_send.at[dx - 1], recv_sem=x_recv.at[dx - 1],
            device_id=(tm, sp_x(dx, sign)), device_id_type=MESH)

    order = (2, 1, 3, 0)
    for dx in order:
        def pack(g, c, dx=dx):
            csend[dx, g] = unit(g, dx, 1 - core).astype(jnp.bfloat16)
            return c
        lax.fori_loop(0, 16, pack, 0)
        core_copy(dx).start()

    for dx in order:
        core_copy(dx).wait_recv()

        def merge(g, c, dx=dx):
            value = unit(g, dx, core) + crecv[dx, g].astype(jnp.float32)
            if dx:
                xsend[dx - 1, g] = value.astype(jnp.bfloat16)
            else:
                part[g] = value
            return c
        lax.fori_loop(0, 16, merge, 0)
        if dx:
            x_copy(dx, 1).start()
    for dx in (1, 2, 3):
        x_copy(dx, -1).wait_recv()

    def merge_x(g, c):
        value = part[g]
        for d in range(3):
            value = value + xrecv[d, g].astype(jnp.float32)
        part[g] = value
        ysend[g] = value.astype(jnp.bfloat16)
        return c
    lax.fori_loop(0, 16, merge_x, 0)

    def y_copy(j, sign):
        t, h = yz_of(j, sign)
        return pltpu.make_async_remote_copy(
            src_ref=ysend.at[t * 2 + h], dst_ref=yrecv.at[j - 1],
            send_sem=y_send.at[j - 1], recv_sem=y_recv.at[j - 1],
            device_id=(t, h * 8 + x * 2 + core), device_id_type=MESH)

    for j in range(1, 16):
        y_copy(j, 1).start()
    total = part[tm * 2 + y_hi]
    for j in range(1, 16):
        y_copy(j, -1).wait_recv()
        total = total + yrecv[j - 1].astype(jnp.float32)
    total = total / cells
    gram_out[:, :half] = total[:8, :]
    gram_out[:, half:] = total[8:, :]

    modes_own.wait()
    for j in range(1, 8):
        modes_copy(j, -1).wait_recv()
        modes_copy(j, 1).wait_send()
    for dx in range(4):
        core_copy(dx).wait_send()
    for dx in (1, 2, 3):
        x_copy(dx, 1).wait_send()
    for j in range(1, 16):
        y_copy(j, 1).wait_send()


def local(snapshots, area_weight, eigvecs, eigvals):
    tm_count = lax.axis_size("tm")
    time_dev, cell_dev = snapshots.shape
    times = time_dev * tm_count
    sub = cell_dev // tm_count
    modes_n = eigvecs.shape[1]
    width = sub // CHUNKS
    vmem = pl.BlockSpec(memory_space=pltpu.VMEM)
    hbm = pl.BlockSpec(memory_space=pltpu.HBM)
    bf16, f32 = jnp.bfloat16, jnp.float32
    half = times // 2
    dma = pltpu.SemaphoreType.DMA
    return pl.pallas_call(
        kernel,
        out_shape=(jax.ShapeDtypeStruct((8, times), f32), jax.ShapeDtypeStruct((8, cell_dev), bf16)),
        in_specs=[hbm] * 4,
        out_specs=(vmem, hbm),
        scratch_shapes=[
            pltpu.VMEM((times, sub), bf16),
            pltpu.VMEM((times, width), bf16),
            pltpu.VMEM((times, times), f32),
            pltpu.VMEM((modes_n, times), bf16),
            pltpu.VMEM((1, modes_n), f32),
            pltpu.VMEM((modes_n, 1), f32),
            pltpu.VMEM((sub // 128, 128), f32),
            pltpu.VMEM((tm_count, 8, sub), bf16),
            pltpu.VMEM((4, 16, 16, half), bf16),
            pltpu.VMEM((4, 16, 16, half), bf16),
            pltpu.VMEM((3, 16, 16, half), bf16),
            pltpu.VMEM((3, 16, 16, half), bf16),
            pltpu.VMEM((16, 16, half), f32),
            pltpu.VMEM((16, 16, half), bf16),
            pltpu.VMEM((15, 16, half), bf16),
            dma((CHUNKS, 7)), dma((CHUNKS, 7)), dma, dma, dma, dma,
            dma((7,)), dma((7,)), dma,
            dma((4,)), dma((4,)), dma((3,)), dma((3,)), dma((15,)), dma((15,)),
        ],
        compiler_params=pltpu.CompilerParams(
            collective_id=0, has_side_effects=True, vmem_limit_bytes=62 << 20),
        cost_estimate=pl.CostEstimate(
            flops=2 * times * times * sub, bytes_accessed=2 * times * sub, transcendentals=0),
    )(snapshots, area_weight.reshape(-1, 128), eigvecs.T, eigvals.reshape(1, -1))


def solution(mesh):
    in_specs = (P("tm", "space"), P("space"), P(), P())
    out_specs = (P(("tm", "space"), None), P("tm", "space"))
    return jax.shard_map(local, mesh=mesh, in_specs=in_specs, out_specs=out_specs, check_vma=False)
```

```python
import jax
import jax.numpy as jnp
from jax import lax
from jax.experimental import pallas as pl
from jax.experimental.pallas import tpu as pltpu
from jax.sharding import PartitionSpec as P

MESH = pl.DeviceIdType.MESH
CHUNKS = 12
AHEAD = 4
FIRST = (1, 2, 3, 4, 5, 7)
LAST = 6
BF16, F32 = jnp.bfloat16, jnp.float32


def kernel(snap, area, evt_in, evals_in, gram_out, modes_out,
           buf, abuf, sbuf, asum, asum_in, means, acc, late, lrow, evt, evals, inv, area_v, mpart, msend,
           csend, crecv, xsend, xrecv, part, ysend, yrecv,
           ltc, ltc_in, lrc, lrc_in, ltx, ltx_in, lrx, lrx_in,
           s_send, s_recv, a_send, a_recv, t_send, t_recv, s_local, m_send, m_recv, m_own,
           c_send, c_recv, x_send, x_recv, y_send, y_recv, lc_send, lc_recv, lx_send, lx_recv):
    time_dev, cell_dev = snap.shape
    times, sub = buf.shape
    width = sub // CHUNKS
    modes_n = evt.shape[0]
    cells = cell_dev * 16
    half = times // 2

    tm = lax.axis_index("tm")
    sp = lax.axis_index("space")
    y_lo, z = tm // 4, lax.rem(tm, 4)
    y_hi, x, core = sp // 8, lax.rem(sp // 2, 4), lax.rem(sp, 2)

    def tm_of(j, sign):
        return lax.rem(y_lo + j // 4, 2) * 4 + lax.rem(z + sign * (j % 4) + 4, 4)

    def sp_x(dx, sign):
        return y_hi * 8 + lax.rem(x + sign * dx + 4, 4) * 2 + core

    def yz_of(j, sign):
        return tm_of(j % 8, sign), lax.rem(y_hi + j // 8, 2)

    def yz_dev(j, sign):
        t, h = yz_of(j, sign)
        return (t, h * 8 + x * 2 + core)

    def rcopy(src, dst, send, recv, device):
        return pltpu.make_async_remote_copy(
            src_ref=src, dst_ref=dst, send_sem=send, recv_sem=recv,
            device_id=device, device_id_type=MESH)

    other = (tm, sp + 1 - 2 * core)
    anti = tm_of(LAST, 1)

    barrier = pltpu.get_barrier_semaphore()
    partners = [yz_dev(j, 1) for j in range(1, 16)] + [other] + [(tm, sp_x(d, 1)) for d in (1, 2, 3)]
    for device in partners:
        pl.semaphore_signal(barrier, inc=1, device_id=device, device_id_type=MESH)
    pl.semaphore_wait(barrier, len(partners))

    def columns(k):
        return pl.ds(pl.multiple_of(k * width, 128), width)

    def block_rows(t):
        return pl.ds(pl.multiple_of(t * time_dev, 128), time_dev)

    def raw(k, i, sign):
        peer = tm_of(FIRST[i], sign)
        row = tm if sign > 0 else peer
        return rcopy(snap.at[:, pl.ds(pl.multiple_of(peer * sub + k * width, 128), width)],
                     buf.at[block_rows(row), columns(k)],
                     s_send.at[k, i], s_recv.at[k, i], (peer, sp))

    def raw_anti(k):
        return rcopy(snap.at[:, pl.ds(pl.multiple_of(anti * sub + k * width, 128), width)],
                     abuf.at[:, columns(k)], a_send.at[k], a_recv.at[k], (anti, sp))

    def start_chunk(k):
        for i in range(len(FIRST)):
            raw(k, i, 1).start()

    area_rows = sub // 128
    local_copies = [pltpu.make_async_copy(src, dst, s_local.at[i]) for i, (src, dst) in enumerate((
        (snap.at[:, pl.ds(pl.multiple_of(anti * sub, 128), sub)], sbuf),
        (snap.at[:, pl.ds(pl.multiple_of(tm * sub, 128), sub)], buf.at[block_rows(tm), :]),
        (area.at[pl.ds(pl.multiple_of(tm * area_rows, 8), area_rows), :], area_v),
        (evals_in, evals),
        (evt_in, evt),
    ))]
    start_chunk(0)
    for copy in local_copies:
        copy.start()
    for k in range(1, AHEAD):
        start_chunk(k)

    local_copies[0].wait()

    def share(k, c):
        asum[:, columns(k)] = jnp.sum(sbuf[:, columns(k)].astype(F32), axis=0, keepdims=True)
        return c
    lax.fori_loop(0, CHUNKS, share, 0)
    sum_copy = rcopy(asum, asum_in, t_send, t_recv, (anti, sp))
    sum_copy.start()

    acc[...] = jnp.zeros_like(acc)
    late[...] = jnp.zeros_like(late)

    def clear(i, c):
        buf[pl.ds(pl.multiple_of(anti * time_dev + i * 16, 16), 16), :] = jnp.zeros((16, sub), BF16)
        return c
    lax.fori_loop(0, time_dev // 16, clear, 0)
    for copy in local_copies[1:]:
        copy.wait()
    eye = lax.broadcasted_iota(jnp.int32, (modes_n, modes_n), 0) == lax.broadcasted_iota(
        jnp.int32, (modes_n, modes_n), 1)
    inv[...] = 1.0 / jnp.sqrt(jnp.sum(
        jnp.where(eye, jnp.broadcast_to(evals[...], (modes_n, modes_n)), 0.0), axis=1, keepdims=True))
    area_v[...] = jnp.sqrt(area_v[...])
    sum_copy.wait_recv()

    strips = width // 128

    def root_of(k):
        return jnp.concatenate([area_v[pl.ds(k * strips + s, 1), :] for s in range(strips)], axis=1)

    def nt_dot(a, b):
        return lax.dot_general(a, b, (((1,), (1,)), ((), ())), preferred_element_type=F32)

    def early_chunk(k, carry):
        for i in range(len(FIRST)):
            raw(k, i, -1).wait_recv()
        for i in range(len(FIRST)):
            raw(k, i, 1).wait_send()

        @pl.when(k + AHEAD < CHUNKS)
        def _():
            start_chunk(k + AHEAD)

        @pl.when(k + AHEAD >= CHUNKS)
        def _():
            raw_anti(k + AHEAD - CHUNKS).start()

        cols = columns(k)
        pieces = (times - time_dev) // 64

        def rows_of(i):
            return pl.ds(pl.multiple_of(lax.rem((anti + 1) * time_dev + i * 64, times), 64), 64)

        def add(i, total):
            block = buf[rows_of(i), cols].astype(F32)
            return total + jnp.sum(block.reshape(8, 8, width), axis=0)

        total = lax.fori_loop(0, pieces, add, jnp.zeros((8, width), F32))
        mean = (jnp.sum(total, axis=0, keepdims=True) + asum_in[:, cols]) / times
        means[:, cols] = mean
        root = root_of(k)

        def weigh(i, c):
            rows = rows_of(i)
            buf[rows, cols] = (root * (buf[rows, cols].astype(F32) - mean)).astype(BF16)
            return c
        lax.fori_loop(0, pieces, weigh, 0)

        def gram(i, c):
            tile = pl.ds(pl.multiple_of(i * 256, 256), 256)
            acc[:, tile] += nt_dot(buf[:, cols], buf[tile, cols])
            return c
        lax.fori_loop(0, times // 256, gram, 0)
        mpart[:, cols] = jnp.dot(evt[...], buf[:, cols], preferred_element_type=F32)
        return carry

    def late_chunk(k, carry):
        raw_anti(k).wait_recv()
        raw_anti(k).wait_send()

        @pl.when(k + AHEAD < CHUNKS)
        def _():
            raw_anti(k + AHEAD).start()

        cols = columns(k)
        weighted = (root_of(k) * (abuf[:, cols].astype(F32) - means[:, cols])).astype(BF16)
        buf[block_rows(anti), cols] = weighted
        late[...] += nt_dot(buf[:, cols], weighted)
        proj = mpart[:, cols] + jnp.dot(
            evt[:, block_rows(anti)], weighted, preferred_element_type=F32)
        proj = (proj * inv[...]).astype(BF16)
        for p in range(8):
            msend[p, :, cols] = proj[p * 8:p * 8 + 8, :]
        return carry

    def unit(ref, g, dx, which):
        at = ((g * 4 + lax.rem(x + dx, 4)) * 2 + which) * 8
        rows = ref[pl.ds(pl.multiple_of(at, 8), 8), :]
        return jnp.concatenate([rows[:, :half], rows[:, half:]], axis=0)

    def narrow(g, dx, which):
        at = ((g * 4 + lax.rem(x + dx, 4)) * 2 + which) * 8
        return late[pl.ds(pl.multiple_of(at, 8), 8), :]

    def core_copy(dx):
        return rcopy(csend.at[dx], crecv.at[dx], c_send.at[dx], c_recv.at[dx], other)

    def x_copy(dx, sign):
        return rcopy(xsend.at[dx - 1], xrecv.at[dx - 1], x_send.at[dx - 1], x_recv.at[dx - 1],
                     (tm, sp_x(dx, sign)))

    lax.fori_loop(0, CHUNKS, early_chunk, 0)

    order = (2, 1, 3, 0)
    for dx in order:
        def pack(g, c, dx=dx):
            csend[dx, g] = unit(acc, g, dx, 1 - core).astype(BF16)
            return c
        lax.fori_loop(0, 16, pack, 0)
        core_copy(dx).start()

    lax.fori_loop(0, 2, late_chunk, 0)

    for dx in order:
        core_copy(dx).wait_recv()

        def merge(g, c, dx=dx):
            value = unit(acc, g, dx, core) + crecv[dx, g].astype(F32)
            if dx:
                xsend[dx - 1, g] = value.astype(BF16)
            else:
                part[g] = value
            return c
        lax.fori_loop(0, 16, merge, 0)
        if dx:
            x_copy(dx, 1).start()

    lax.fori_loop(2, 9, late_chunk, 0)

    for dx in (1, 2, 3):
        x_copy(dx, -1).wait_recv()

    def merge_x(g, c):
        value = part[g]
        for d in range(3):
            value = value + xrecv[d, g].astype(F32)
        part[g] = value
        return c
    lax.fori_loop(0, 16, merge_x, 0)

    lax.fori_loop(9, CHUNKS, late_chunk, 0)

    def modes_copy(j, sign):
        peer = tm_of(j, sign)
        col = tm if sign > 0 else peer
        return rcopy(msend.at[peer], modes_out.at[:, pl.ds(pl.multiple_of(col * sub, 128), sub)],
                     m_send.at[j - 1], m_recv.at[j - 1], (peer, sp))

    for j in range(1, 8):
        modes_copy(j, 1).start()
    modes_own = pltpu.make_async_copy(
        msend.at[tm], modes_out.at[:, pl.ds(pl.multiple_of(tm * sub, 128), sub)], m_own)
    modes_own.start()

    lt_core = rcopy(ltc, ltc_in, lc_send.at[0], lc_recv.at[0], other)
    lr_core = rcopy(lrc, lrc_in, lc_send.at[1], lc_recv.at[1], other)

    def lt_x(dx, sign):
        return rcopy(ltx.at[dx - 1], ltx_in.at[dx - 1], lx_send.at[0, dx - 1], lx_recv.at[0, dx - 1],
                     (tm, sp_x(dx, sign)))

    def lr_x(dx, sign):
        return rcopy(lrx.at[dx - 1], lrx_in.at[dx - 1], lx_send.at[1, dx - 1], lx_recv.at[1, dx - 1],
                     (tm, sp_x(dx, sign)))

    def lt_pack(g, c):
        for dx in range(4):
            ltc[dx, g] = narrow(g, dx, 1 - core).astype(BF16)
        return c
    lax.fori_loop(0, 16, lt_pack, 0)
    lt_core.start()

    def turn(i, c):
        t = lax.rem(anti + 1 + i, 8)
        lrow[:, block_rows(t)] = jnp.transpose(late[block_rows(t), :])
        return c
    lax.fori_loop(0, 7, turn, 0)
    lrow[:, block_rows(anti)] = jnp.zeros((time_dev, time_dev), F32)
    for dx in range(4):
        for h in range(2):
            lrc[dx, h] = unit(lrow, h, dx, 1 - core).astype(BF16)
    lr_core.start()

    lane = pl.ds(pl.multiple_of(lax.rem(anti, 4) * 128, 128), 128)
    top = pl.ds(pl.multiple_of((anti // 4) * 8, 8), 8)

    lt_core.wait_recv()
    for dx in order:
        def lt_merge(g, c, dx=dx):
            value = narrow(g, dx, core) + ltc_in[dx, g].astype(F32)
            if dx:
                ltx[dx - 1, g] = value.astype(BF16)
            else:
                part[g, top, lane] += value
            return c
        lax.fori_loop(0, 16, lt_merge, 0)
        if dx:
            lt_x(dx, 1).start()
    lr_core.wait_recv()
    for dx in order:
        for h in range(2):
            value = unit(lrow, h, dx, core) + lrc_in[dx, h].astype(F32)
            if dx:
                lrx[dx - 1, h] = value.astype(BF16)
            else:
                part[anti * 2 + h] += value
        if dx:
            lr_x(dx, 1).start()
    for dx in (1, 2, 3):
        lt_x(dx, -1).wait_recv()

    def lt_sum(g, c):
        value = part[g, top, lane]
        for d in range(3):
            value = value + ltx_in[d, g].astype(F32)
        part[g, top, lane] = value
        return c
    lax.fori_loop(0, 16, lt_sum, 0)
    for dx in (1, 2, 3):
        lr_x(dx, -1).wait_recv()
    for h in range(2):
        value = part[anti * 2 + h]
        for d in range(3):
            value = value + lrx_in[d, h].astype(F32)
        part[anti * 2 + h] = value

    def y_copy(j, sign):
        t, h = yz_of(j, sign)
        return rcopy(ysend.at[t * 2 + h], yrecv.at[j - 1], y_send.at[j - 1], y_recv.at[j - 1],
                     (t, h * 8 + x * 2 + core))

    def y_pack(g, c):
        ysend[g] = part[g].astype(BF16)
        return c
    lax.fori_loop(0, 16, y_pack, 0)
    for j in range(1, 16):
        y_copy(j, 1).start()
    total = part[tm * 2 + y_hi]
    for j in range(1, 16):
        y_copy(j, -1).wait_recv()
        total = total + yrecv[j - 1].astype(F32)
    total = total / cells
    gram_out[:, :half] = total[:8, :]
    gram_out[:, half:] = total[8:, :]

    modes_own.wait()
    sum_copy.wait_send()
    for j in range(1, 8):
        modes_copy(j, -1).wait_recv()
        modes_copy(j, 1).wait_send()
    for dx in range(4):
        core_copy(dx).wait_send()
    lt_core.wait_send()
    lr_core.wait_send()
    for dx in (1, 2, 3):
        x_copy(dx, 1).wait_send()
        lt_x(dx, 1).wait_send()
        lr_x(dx, 1).wait_send()
    for j in range(1, 16):
        y_copy(j, 1).wait_send()


def local(snapshots, area_weight, eigvecs, eigvals):
    tm_count = lax.axis_size("tm")
    time_dev, cell_dev = snapshots.shape
    times = time_dev * tm_count
    sub = cell_dev // tm_count
    modes_n = eigvecs.shape[1]
    half = times // 2
    vmem = pl.BlockSpec(memory_space=pltpu.VMEM)
    hbm = pl.BlockSpec(memory_space=pltpu.HBM)
    dma = pltpu.SemaphoreType.DMA
    return pl.pallas_call(
        kernel,
        out_shape=(jax.ShapeDtypeStruct((8, times), F32), jax.ShapeDtypeStruct((8, cell_dev), BF16)),
        in_specs=[hbm] * 4,
        out_specs=(vmem, hbm),
        scratch_shapes=[
            pltpu.VMEM((times, sub), BF16),
            pltpu.VMEM((time_dev, sub), BF16),
            pltpu.VMEM((time_dev, sub), BF16),
            pltpu.VMEM((1, sub), F32),
            pltpu.VMEM((1, sub), F32),
            pltpu.VMEM((1, sub), F32),
            pltpu.VMEM((times, times), F32),
            pltpu.VMEM((times, time_dev), F32),
            pltpu.VMEM((time_dev, times), F32),
            pltpu.VMEM((modes_n, times), BF16),
            pltpu.VMEM((1, modes_n), F32),
            pltpu.VMEM((modes_n, 1), F32),
            pltpu.VMEM((sub // 128, 128), F32),
            pltpu.VMEM((modes_n, sub), F32),
            pltpu.VMEM((tm_count, 8, sub), BF16),
            pltpu.VMEM((4, 16, 16, half), BF16),
            pltpu.VMEM((4, 16, 16, half), BF16),
            pltpu.VMEM((3, 16, 16, half), BF16),
            pltpu.VMEM((3, 16, 16, half), BF16),
            pltpu.VMEM((16, 16, half), F32),
            pltpu.VMEM((16, 16, half), BF16),
            pltpu.VMEM((15, 16, half), BF16),
            pltpu.VMEM((4, 16, 8, 128), BF16),
            pltpu.VMEM((4, 16, 8, 128), BF16),
            pltpu.VMEM((4, 2, 16, half), BF16),
            pltpu.VMEM((4, 2, 16, half), BF16),
            pltpu.VMEM((3, 16, 8, 128), BF16),
            pltpu.VMEM((3, 16, 8, 128), BF16),
            pltpu.VMEM((3, 2, 16, half), BF16),
            pltpu.VMEM((3, 2, 16, half), BF16),
            dma((CHUNKS, len(FIRST))), dma((CHUNKS, len(FIRST))), dma((CHUNKS,)), dma((CHUNKS,)),
            dma, dma, dma((5,)), dma((7,)), dma((7,)), dma,
            dma((4,)), dma((4,)), dma((3,)), dma((3,)), dma((15,)), dma((15,)),
            dma((2,)), dma((2,)), dma((2, 3)), dma((2, 3)),
        ],
        compiler_params=pltpu.CompilerParams(
            collective_id=0, has_side_effects=True, vmem_limit_bytes=48 << 20),
        cost_estimate=pl.CostEstimate(
            flops=2 * times * times * sub, bytes_accessed=2 * times * sub, transcendentals=0),
    )(*[pltpu.with_memory_space_constraint(v, pltpu.HBM) for v in (
        snapshots, area_weight.reshape(-1, 128), eigvecs.T, eigvals.reshape(1, -1))])


def solution(mesh):
    in_specs = (P("tm", "space"), P("space"), P(), P())
    out_specs = (P(("tm", "space"), None), P("tm", "space"))
    return jax.shard_map(local, mesh=mesh, in_specs=in_specs, out_specs=out_specs, check_vma=False)
```

```python
import jax
import jax.numpy as jnp
from jax import lax
from jax.experimental import pallas as pl
from jax.experimental.pallas import tpu as pltpu
from jax.sharding import PartitionSpec as P

MESH = pl.DeviceIdType.MESH
CHUNKS = 12
AHEAD = 6
FIRST = (1, 2, 3, 4, 5, 7)
LAST = 6
BF16, F32 = jnp.bfloat16, jnp.float32


def kernel(snap, area, evt_in, evals_in, gram_out, modes_out,
           buf, abuf, sbuf, asum, asum_in, means, acc, late, lrow, evt, evals, inv, area_v, mpart, msend,
           csend, crecv, xsend, xrecv, part, osend, orecv, opart, isend, irecv, zsend, zrecv,
           ltc, ltc_in, lrc, lrc_in, ltx, ltx_in, lrx, lrx_in,
           lt_part, lr_part, lty, lty_in, lry, lry_in, final,
           s_send, s_recv, a_send, a_recv, t_send, t_recv, s_local, m_send, m_recv, m_own,
           c_send, c_recv, x_send, x_recv, o_send, o_recv, z_send, z_recv, lc_send, lc_recv, lx_send, lx_recv,
           ly_send, ly_recv, lry_send, lry_recv):
    time_dev, cell_dev = snap.shape
    times, sub = buf.shape
    width = sub // CHUNKS
    modes_n = evt.shape[0]
    cells = cell_dev * 16
    half = times // 2

    tm = lax.axis_index("tm")
    sp = lax.axis_index("space")
    y_lo, z = tm // 4, lax.rem(tm, 4)
    y_hi, x, core = sp // 8, lax.rem(sp // 2, 4), lax.rem(sp, 2)

    def tm_of(j, sign):
        return lax.rem(y_lo + j // 4, 2) * 4 + lax.rem(z + sign * (j % 4) + 4, 4)

    def sp_x(dx, sign):
        return y_hi * 8 + lax.rem(x + sign * dx + 4, 4) * 2 + core

    def yz_of(j, sign):
        return tm_of(j % 8, sign), lax.rem(y_hi + j // 8, 2)

    def yz_dev(j, sign):
        t, h = yz_of(j, sign)
        return (t, h * 8 + x * 2 + core)

    def rcopy(src, dst, send, recv, device):
        return pltpu.make_async_remote_copy(
            src_ref=src, dst_ref=dst, send_sem=send, recv_sem=recv,
            device_id=device, device_id_type=MESH)

    other = (tm, sp + 1 - 2 * core)
    anti = tm_of(LAST, 1)

    barrier = pltpu.get_barrier_semaphore()
    partners = [yz_dev(j, 1) for j in range(1, 16)] + [other] + [(tm, sp_x(d, 1)) for d in (1, 2, 3)]
    for device in partners:
        pl.semaphore_signal(barrier, inc=1, device_id=device, device_id_type=MESH)
    pl.semaphore_wait(barrier, len(partners))

    def columns(k):
        return pl.ds(pl.multiple_of(k * width, 128), width)

    def block_rows(t):
        return pl.ds(pl.multiple_of(t * time_dev, 128), time_dev)

    def raw(k, i, sign):
        peer = tm_of(FIRST[i], sign)
        row = tm if sign > 0 else peer
        return rcopy(snap.at[:, pl.ds(pl.multiple_of(peer * sub + k * width, 128), width)],
                     buf.at[block_rows(row), columns(k)],
                     s_send.at[k, i], s_recv.at[k, i], (peer, sp))

    def raw_anti(k):
        return rcopy(snap.at[:, pl.ds(pl.multiple_of(anti * sub + k * width, 128), width)],
                     abuf.at[:, columns(k)], a_send.at[k], a_recv.at[k], (anti, sp))

    def start_chunk(k):
        for i in range(len(FIRST)):
            raw(k, i, 1).start()

    area_rows = sub // 128
    local_copies = [pltpu.make_async_copy(src, dst, s_local.at[i]) for i, (src, dst) in enumerate((
        (snap.at[:, pl.ds(pl.multiple_of(anti * sub, 128), sub)], sbuf),
        (snap.at[:, pl.ds(pl.multiple_of(tm * sub, 128), sub)], buf.at[block_rows(tm), :]),
        (area.at[pl.ds(pl.multiple_of(tm * area_rows, 8), area_rows), :], area_v),
        (evals_in, evals),
        (evt_in, evt),
    ))]
    start_chunk(0)
    for copy in local_copies:
        copy.start()

    local_copies[0].wait()

    def share(k, c):
        asum[:, columns(k)] = jnp.sum(sbuf[:, columns(k)].astype(F32), axis=0, keepdims=True)
        return c
    lax.fori_loop(0, CHUNKS, share, 0)
    sum_copy = rcopy(asum, asum_in, t_send, t_recv, (anti, sp))
    sum_copy.start()
    for k in range(1, AHEAD):
        start_chunk(k)

    acc[...] = jnp.zeros_like(acc)
    late[...] = jnp.zeros_like(late)

    def clear(i, c):
        buf[pl.ds(pl.multiple_of(anti * time_dev + i * 16, 16), 16), :] = jnp.zeros((16, sub), BF16)
        return c
    lax.fori_loop(0, time_dev // 16, clear, 0)
    for copy in local_copies[1:]:
        copy.wait()
    eye = lax.broadcasted_iota(jnp.int32, (modes_n, modes_n), 0) == lax.broadcasted_iota(
        jnp.int32, (modes_n, modes_n), 1)
    inv[...] = 1.0 / jnp.sqrt(jnp.sum(
        jnp.where(eye, jnp.broadcast_to(evals[...], (modes_n, modes_n)), 0.0), axis=1, keepdims=True))
    area_v[...] = jnp.sqrt(area_v[...])
    sum_copy.wait_recv()

    strips = width // 128

    def root_of(k):
        return jnp.concatenate([area_v[pl.ds(k * strips + s, 1), :] for s in range(strips)], axis=1)

    def nt_dot(a, b):
        return lax.dot_general(a, b, (((1,), (1,)), ((), ())), preferred_element_type=F32)

    def early_chunk(k, carry):
        for i in range(len(FIRST)):
            raw(k, i, -1).wait_recv()
        for i in range(len(FIRST)):
            raw(k, i, 1).wait_send()

        @pl.when(k + AHEAD < CHUNKS)
        def _():
            start_chunk(k + AHEAD)

        @pl.when(k + AHEAD >= CHUNKS)
        def _():
            raw_anti(k + AHEAD - CHUNKS).start()

        cols = columns(k)
        pieces = (times - time_dev) // 64

        def rows_of(i):
            return pl.ds(pl.multiple_of(lax.rem((anti + 1) * time_dev + i * 64, times), 64), 64)

        def add(i, total):
            block = buf[rows_of(i), cols].astype(F32)
            return total + jnp.sum(block.reshape(8, 8, width), axis=0)

        total = lax.fori_loop(0, pieces, add, jnp.zeros((8, width), F32))
        mean = (jnp.sum(total, axis=0, keepdims=True) + asum_in[:, cols]) / times
        means[:, cols] = mean
        root = root_of(k)

        def weigh(i, c):
            rows = rows_of(i)
            buf[rows, cols] = (root * (buf[rows, cols].astype(F32) - mean)).astype(BF16)
            return c
        lax.fori_loop(0, pieces, weigh, 0)

        def gram(i, c):
            tile = pl.ds(pl.multiple_of(i * 256, 256), 256)
            acc[:, tile] += nt_dot(buf[:, cols], buf[tile, cols])
            return c
        lax.fori_loop(0, times // 256, gram, 0)
        mpart[:, cols] = jnp.dot(evt[...], buf[:, cols], preferred_element_type=F32)
        return carry

    def late_chunk(k, carry):
        raw_anti(k).wait_recv()
        raw_anti(k).wait_send()

        @pl.when(k + AHEAD < CHUNKS)
        def _():
            raw_anti(k + AHEAD).start()

        cols = columns(k)
        weighted = (root_of(k) * (abuf[:, cols].astype(F32) - means[:, cols])).astype(BF16)
        buf[block_rows(anti), cols] = weighted
        late[...] += nt_dot(buf[:, cols], weighted)
        proj = mpart[:, cols] + jnp.dot(
            evt[:, block_rows(anti)], weighted, preferred_element_type=F32)
        proj = (proj * inv[...]).astype(BF16)
        for p in range(8):
            msend[p, :, cols] = proj[p * 8:p * 8 + 8, :]
        return carry

    def unit(ref, g, dx, which):
        at = ((g * 4 + lax.rem(x + dx, 4)) * 2 + which) * 8
        rows = ref[pl.ds(pl.multiple_of(at, 8), 8), :]
        return jnp.concatenate([rows[:, :half], rows[:, half:]], axis=0)

    def narrow(g, dx, which):
        at = ((g * 4 + lax.rem(x + dx, 4)) * 2 + which) * 8
        return late[pl.ds(pl.multiple_of(at, 8), 8), :]

    def core_copy(dx):
        return rcopy(csend.at[dx], crecv.at[dx], c_send.at[dx], c_recv.at[dx], other)

    def x_copy(dx, sign):
        return rcopy(xsend.at[dx - 1], xrecv.at[dx - 1], x_send.at[dx - 1], x_recv.at[dx - 1],
                     (tm, sp_x(dx, sign)))

    lax.fori_loop(0, CHUNKS, early_chunk, 0)

    order = (2, 1, 3, 0)
    for dx in order:
        def pack(g, c, dx=dx):
            csend[dx, g] = unit(acc, g, dx, 1 - core).astype(BF16)
            return c
        lax.fori_loop(0, 16, pack, 0)
        core_copy(dx).start()

    lax.fori_loop(0, 1, late_chunk, 0)

    for dx in order:
        core_copy(dx).wait_recv()

        def merge(g, c, dx=dx):
            value = unit(acc, g, dx, core) + crecv[dx, g].astype(F32)
            if dx:
                xsend[dx - 1, g] = value.astype(BF16)
            else:
                part[g] = value
            return c
        lax.fori_loop(0, 16, merge, 0)
        if dx:
            x_copy(dx, 1).start()

    lax.fori_loop(1, 7, late_chunk, 0)

    for dx in (1, 2, 3):
        x_copy(dx, -1).wait_recv()

    outer = (tm_of(4, 1), (1 - y_hi) * 8 + x * 2 + core)
    inner = (tm_of(4, 1), sp)
    o_copy = rcopy(osend, orecv, o_send.at[0], o_recv.at[0], outer)
    i_copy = rcopy(isend, irecv, o_send.at[1], o_recv.at[1], inner)

    def x_total(g):
        value = part[g]
        for d in range(3):
            value = value + xrecv[d, g].astype(F32)
        return value

    def merge_x(t, c):
        osend[t] = x_total(t * 2 + 1 - y_hi).astype(BF16)
        return c
    lax.fori_loop(0, 8, merge_x, 0)
    o_copy.start()

    def merge_own(t, c):
        opart[t] = x_total(t * 2 + y_hi)
        return c
    lax.fori_loop(0, 8, merge_own, 0)

    lax.fori_loop(7, 8, late_chunk, 0)

    o_copy.wait_recv()

    def merge_o(t, c):
        other_t = (1 - y_lo) * 4 + t
        isend[t] = (opart[other_t] + orecv[other_t].astype(F32)).astype(BF16)
        return c
    lax.fori_loop(0, 4, merge_o, 0)
    i_copy.start()

    lax.fori_loop(8, 10, late_chunk, 0)

    i_copy.wait_recv()

    def y_total(t):
        own_t = y_lo * 4 + t
        return opart[own_t] + orecv[own_t].astype(F32) + irecv[t].astype(F32)

    def merge_i(t, c):
        zsend[t] = y_total(t).astype(BF16)
        return c
    lax.fori_loop(0, 4, merge_i, 0)

    def z_copy(dz, sign):
        peer = tm_of(dz, sign)
        return rcopy(zsend.at[lax.rem(peer, 4)], zrecv.at[dz - 1], z_send.at[dz - 1], z_recv.at[dz - 1],
                     (peer, sp))
    for dz in (1, 2, 3):
        z_copy(dz, 1).start()
    final_early = y_total(z)
    final[:, :half] = final_early[:8, :]
    final[:, half:] = final_early[8:, :]

    lax.fori_loop(10, CHUNKS, late_chunk, 0)

    def modes_copy(j, sign):
        peer = tm_of(j, sign)
        col = tm if sign > 0 else peer
        return rcopy(msend.at[peer], modes_out.at[:, pl.ds(pl.multiple_of(col * sub, 128), sub)],
                     m_send.at[j - 1], m_recv.at[j - 1], (peer, sp))

    lt_core = rcopy(ltc, ltc_in, lc_send.at[0], lc_recv.at[0], other)
    lr_core = rcopy(lrc, lrc_in, lc_send.at[1], lc_recv.at[1], other)

    def lt_x(dx, sign):
        return rcopy(ltx.at[dx - 1], ltx_in.at[dx - 1], lx_send.at[0, dx - 1], lx_recv.at[0, dx - 1],
                     (tm, sp_x(dx, sign)))

    def lr_x(dx, sign):
        return rcopy(lrx.at[dx - 1], lrx_in.at[dx - 1], lx_send.at[1, dx - 1], lx_recv.at[1, dx - 1],
                     (tm, sp_x(dx, sign)))

    def lt_pack(g, c):
        for dx in range(4):
            ltc[dx, g] = narrow(g, dx, 1 - core).astype(BF16)
        return c
    lax.fori_loop(0, 16, lt_pack, 0)
    lt_core.start()
    for j in range(1, 8):
        modes_copy(j, 1).start()
    modes_own = pltpu.make_async_copy(
        msend.at[tm], modes_out.at[:, pl.ds(pl.multiple_of(tm * sub, 128), sub)], m_own)
    modes_own.start()

    def turn(i, c):
        t = lax.rem(anti + 1 + i, 8)
        lrow[:, block_rows(t)] = jnp.transpose(late[block_rows(t), :])
        return c
    lax.fori_loop(0, 7, turn, 0)
    lrow[:, block_rows(anti)] = jnp.zeros((time_dev, time_dev), F32)
    for dx in range(4):
        for h in range(2):
            lrc[dx, h] = unit(lrow, h, dx, 1 - core).astype(BF16)
    lr_core.start()

    lt_core.wait_recv()
    for dx in order:
        def lt_merge(g, c, dx=dx):
            value = narrow(g, dx, core) + ltc_in[dx, g].astype(F32)
            if dx:
                ltx[dx - 1, g] = value.astype(BF16)
            else:
                lt_part[g] = value
            return c
        lax.fori_loop(0, 16, lt_merge, 0)
        if dx:
            lt_x(dx, 1).start()
    lr_core.wait_recv()
    for dx in order:
        for h in range(2):
            value = unit(lrow, h, dx, core) + lrc_in[dx, h].astype(F32)
            if dx:
                lrx[dx - 1, h] = value.astype(BF16)
            else:
                lr_part[h] = value
        if dx:
            lr_x(dx, 1).start()
    for dx in (1, 2, 3):
        lt_x(dx, -1).wait_recv()

    def lt_sum(g, c):
        value = lt_part[g]
        for d in range(3):
            value = value + ltx_in[d, g].astype(F32)
        lt_part[g] = value
        lty[g] = value.astype(BF16)
        return c
    lax.fori_loop(0, 16, lt_sum, 0)

    def lt_y(j, sign):
        t, h = yz_of(j, sign)
        return rcopy(lty.at[t * 2 + h], lty_in.at[j - 1], ly_send.at[j - 1], ly_recv.at[j - 1],
                     (t, h * 8 + x * 2 + core))

    for j in range(1, 16):
        lt_y(j, 1).start()

    for dx in (1, 2, 3):
        lr_x(dx, -1).wait_recv()
    for h in range(2):
        value = lr_part[h]
        for d in range(3):
            value = value + lrx_in[d, h].astype(F32)
        lry[h] = value.astype(BF16)

    def lr_y(i, sign):
        t, h = yz_of(LAST + 8 * i, sign)
        return rcopy(lry.at[h], lry_in.at[i], lry_send.at[i], lry_recv.at[i],
                     (t, h * 8 + x * 2 + core))

    for i in range(2):
        lr_y(i, 1).start()

    for dz in (1, 2, 3):
        z_copy(dz, -1).wait_recv()
        value = zrecv[dz - 1].astype(F32)
        final[:, :half] += value[:8, :]
        final[:, half:] += value[8:, :]
    final[:, block_rows(anti)] += lt_part[tm * 2 + y_hi]
    for j in range(1, 16):
        lt_y(j, -1).wait_recv()
        facing = (j // 4 + 1) % 2 * 4 + (j + 2) % 4
        final[:, block_rows(tm_of(facing, -1))] += lty_in[j - 1].astype(F32)
    total = jnp.concatenate([final[:, :half], final[:, half:]], axis=0)
    for i in range(2):
        lr_y(i, -1).wait_recv()
        total = total + lry_in[i].astype(F32)
    total = total / cells
    gram_out[:, :half] = total[:8, :]
    gram_out[:, half:] = total[8:, :]

    modes_own.wait()
    sum_copy.wait_send()
    for j in range(1, 8):
        modes_copy(j, -1).wait_recv()
        modes_copy(j, 1).wait_send()
    for dx in range(4):
        core_copy(dx).wait_send()
    lt_core.wait_send()
    lr_core.wait_send()
    o_copy.wait_send()
    i_copy.wait_send()
    for dx in (1, 2, 3):
        x_copy(dx, 1).wait_send()
        z_copy(dx, 1).wait_send()
        lt_x(dx, 1).wait_send()
        lr_x(dx, 1).wait_send()
    for j in range(1, 16):
        lt_y(j, 1).wait_send()
    for i in range(2):
        lr_y(i, 1).wait_send()


def local(snapshots, area_weight, eigvecs, eigvals):
    tm_count = lax.axis_size("tm")
    time_dev, cell_dev = snapshots.shape
    times = time_dev * tm_count
    sub = cell_dev // tm_count
    modes_n = eigvecs.shape[1]
    half = times // 2
    vmem = pl.BlockSpec(memory_space=pltpu.VMEM)
    hbm = pl.BlockSpec(memory_space=pltpu.HBM)
    dma = pltpu.SemaphoreType.DMA
    return pl.pallas_call(
        kernel,
        out_shape=(jax.ShapeDtypeStruct((8, times), F32), jax.ShapeDtypeStruct((8, cell_dev), BF16)),
        in_specs=[hbm] * 4,
        out_specs=(vmem, hbm),
        scratch_shapes=[
            pltpu.VMEM((times, sub), BF16),
            pltpu.VMEM((time_dev, sub), BF16),
            pltpu.VMEM((time_dev, sub), BF16),
            pltpu.VMEM((1, sub), F32),
            pltpu.VMEM((1, sub), F32),
            pltpu.VMEM((1, sub), F32),
            pltpu.VMEM((times, times), F32),
            pltpu.VMEM((times, time_dev), F32),
            pltpu.VMEM((time_dev, times), F32),
            pltpu.VMEM((modes_n, times), BF16),
            pltpu.VMEM((1, modes_n), F32),
            pltpu.VMEM((modes_n, 1), F32),
            pltpu.VMEM((sub // 128, 128), F32),
            pltpu.VMEM((modes_n, sub), F32),
            pltpu.VMEM((tm_count, 8, sub), BF16),
            pltpu.VMEM((4, 16, 16, half), BF16),
            pltpu.VMEM((4, 16, 16, half), BF16),
            pltpu.VMEM((3, 16, 16, half), BF16),
            pltpu.VMEM((3, 16, 16, half), BF16),
            pltpu.VMEM((16, 16, half), F32),
            pltpu.VMEM((8, 16, half), BF16),
            pltpu.VMEM((8, 16, half), BF16),
            pltpu.VMEM((8, 16, half), F32),
            pltpu.VMEM((4, 16, half), BF16),
            pltpu.VMEM((4, 16, half), BF16),
            pltpu.VMEM((4, 16, half), BF16),
            pltpu.VMEM((3, 16, half), BF16),
            pltpu.VMEM((4, 16, 8, 128), BF16),
            pltpu.VMEM((4, 16, 8, 128), BF16),
            pltpu.VMEM((4, 2, 16, half), BF16),
            pltpu.VMEM((4, 2, 16, half), BF16),
            pltpu.VMEM((3, 16, 8, 128), BF16),
            pltpu.VMEM((3, 16, 8, 128), BF16),
            pltpu.VMEM((3, 2, 16, half), BF16),
            pltpu.VMEM((3, 2, 16, half), BF16),
            pltpu.VMEM((16, 8, 128), F32),
            pltpu.VMEM((2, 16, half), F32),
            pltpu.VMEM((16, 8, 128), BF16),
            pltpu.VMEM((15, 8, 128), BF16),
            pltpu.VMEM((2, 16, half), BF16),
            pltpu.VMEM((2, 16, half), BF16),
            pltpu.VMEM((8, times), F32),
            dma((CHUNKS, len(FIRST))), dma((CHUNKS, len(FIRST))), dma((CHUNKS,)), dma((CHUNKS,)),
            dma, dma, dma((5,)), dma((7,)), dma((7,)), dma,
            dma((4,)), dma((4,)), dma((3,)), dma((3,)), dma((2,)), dma((2,)), dma((3,)), dma((3,)),
            dma((2,)), dma((2,)), dma((2, 3)), dma((2, 3)),
            dma((15,)), dma((15,)), dma((2,)), dma((2,)),
        ],
        compiler_params=pltpu.CompilerParams(
            collective_id=0, has_side_effects=True, vmem_limit_bytes=48 << 20),
        cost_estimate=pl.CostEstimate(
            flops=2 * times * times * sub, bytes_accessed=2 * times * sub, transcendentals=0),
    )(*[pltpu.with_memory_space_constraint(v, pltpu.HBM) for v in (
        snapshots, area_weight.reshape(-1, 128), eigvecs.T, eigvals.reshape(1, -1))])


def solution(mesh):
    in_specs = (P("tm", "space"), P("space"), P(), P())
    out_specs = (P(("tm", "space"), None), P("tm", "space"))
    return jax.shard_map(local, mesh=mesh, in_specs=in_specs, out_specs=out_specs, check_vma=False)
```

```python
import jax
import jax.numpy as jnp
from jax import lax
from jax.experimental import pallas as pl
from jax.experimental.pallas import tpu as pltpu
from jax.sharding import PartitionSpec as P

MESH = pl.DeviceIdType.MESH
CHUNKS = 12
AHEAD = 6
FIRST = (1, 2, 3, 4, 5, 7)
LAST = 6
BF16, F32 = jnp.bfloat16, jnp.float32


def kernel(snap, area, evt_in, evals_in, gram_out, modes_out,
           buf, abuf, sbuf, asum, asum_in, means, acc, late, lrow, evt, evals, inv, area_v, mpart, msend,
           csend, crecv, xsend, xrecv, part, osend, orecv, opart, isend, irecv, zsend, zrecv,
           ltc, ltc_in, lrc, lrc_in, ltx, ltx_in, lrx, lrx_in,
           lt_part, lr_part, lty, lty_in, lry, lry_in, final,
           s_send, s_recv, a_send, a_recv, t_send, t_recv, s_local, m_send, m_recv, m_own,
           c_send, c_recv, x_send, x_recv, o_send, o_recv, z_send, z_recv, lc_send, lc_recv, lx_send, lx_recv,
           ly_send, ly_recv, lry_send, lry_recv):
    time_dev, cell_dev = snap.shape
    times, sub = buf.shape
    width = sub // CHUNKS
    modes_n = evt.shape[0]
    cells = cell_dev * 16
    half = times // 2

    tm = lax.axis_index("tm")
    sp = lax.axis_index("space")
    y_lo, z = tm // 4, lax.rem(tm, 4)
    y_hi, x, core = sp // 8, lax.rem(sp // 2, 4), lax.rem(sp, 2)

    def tm_of(j, sign):
        return lax.rem(y_lo + j // 4, 2) * 4 + lax.rem(z + sign * (j % 4) + 4, 4)

    def sp_x(dx, sign):
        return y_hi * 8 + lax.rem(x + sign * dx + 4, 4) * 2 + core

    def yz_of(j, sign):
        return tm_of(j % 8, sign), lax.rem(y_hi + j // 8, 2)

    def yz_dev(j, sign):
        t, h = yz_of(j, sign)
        return (t, h * 8 + x * 2 + core)

    def rcopy(src, dst, send, recv, device):
        return pltpu.make_async_remote_copy(
            src_ref=src, dst_ref=dst, send_sem=send, recv_sem=recv,
            device_id=device, device_id_type=MESH)

    other = (tm, sp + 1 - 2 * core)
    anti = tm_of(LAST, 1)

    barrier = pltpu.get_barrier_semaphore()
    partners = [yz_dev(j, 1) for j in range(1, 16)] + [other] + [(tm, sp_x(d, 1)) for d in (1, 2, 3)]
    for device in partners:
        pl.semaphore_signal(barrier, inc=1, device_id=device, device_id_type=MESH)
    pl.semaphore_wait(barrier, len(partners))

    def columns(k):
        return pl.ds(pl.multiple_of(k * width, 128), width)

    def block_rows(t):
        return pl.ds(pl.multiple_of(t * time_dev, 128), time_dev)

    def raw(k, i, sign):
        peer = tm_of(FIRST[i], sign)
        row = tm if sign > 0 else peer
        return rcopy(snap.at[:, pl.ds(pl.multiple_of(peer * sub + k * width, 128), width)],
                     buf.at[block_rows(row), columns(k)],
                     s_send.at[k, i], s_recv.at[k, i], (peer, sp))

    def raw_anti(k):
        return rcopy(snap.at[:, pl.ds(pl.multiple_of(anti * sub + k * width, 128), width)],
                     abuf.at[:, columns(k)], a_send.at[k], a_recv.at[k], (anti, sp))

    def start_chunk(k):
        for i in range(len(FIRST)):
            raw(k, i, 1).start()

    area_rows = sub // 128
    local_copies = [pltpu.make_async_copy(src, dst, s_local.at[i]) for i, (src, dst) in enumerate((
        (snap.at[:, pl.ds(pl.multiple_of(anti * sub, 128), sub)], sbuf),
        (snap.at[:, pl.ds(pl.multiple_of(tm * sub, 128), sub)], buf.at[block_rows(tm), :]),
        (area.at[pl.ds(pl.multiple_of(tm * area_rows, 8), area_rows), :], area_v),
        (evals_in, evals),
        (evt_in, evt),
    ))]
    start_chunk(0)
    for copy in local_copies:
        copy.start()

    local_copies[0].wait()

    def share(k, c):
        asum[:, columns(k)] = jnp.sum(sbuf[:, columns(k)].astype(F32), axis=0, keepdims=True)
        return c
    lax.fori_loop(0, CHUNKS, share, 0)
    sum_copy = rcopy(asum, asum_in, t_send, t_recv, (anti, sp))
    sum_copy.start()
    for k in range(1, AHEAD):
        start_chunk(k)

    acc[...] = jnp.zeros_like(acc)
    late[...] = jnp.zeros_like(late)

    def clear(i, c):
        buf[pl.ds(pl.multiple_of(anti * time_dev + i * 16, 16), 16), :] = jnp.zeros((16, sub), BF16)
        return c
    lax.fori_loop(0, time_dev // 16, clear, 0)
    for copy in local_copies[1:]:
        copy.wait()
    eye = lax.broadcasted_iota(jnp.int32, (modes_n, modes_n), 0) == lax.broadcasted_iota(
        jnp.int32, (modes_n, modes_n), 1)
    inv[...] = 1.0 / jnp.sqrt(jnp.sum(
        jnp.where(eye, jnp.broadcast_to(evals[...], (modes_n, modes_n)), 0.0), axis=1, keepdims=True))
    area_v[...] = jnp.sqrt(area_v[...])
    sum_copy.wait_recv()

    strips = width // 128

    def root_of(k):
        return jnp.concatenate([area_v[pl.ds(k * strips + s, 1), :] for s in range(strips)], axis=1)

    def nt_dot(a, b):
        return lax.dot_general(a, b, (((1,), (1,)), ((), ())), preferred_element_type=F32)

    def early_chunk(k, carry):
        for i in range(len(FIRST)):
            raw(k, i, -1).wait_recv()
        for i in range(len(FIRST)):
            raw(k, i, 1).wait_send()

        @pl.when(k + AHEAD < CHUNKS)
        def _():
            start_chunk(k + AHEAD)

        @pl.when(k + AHEAD >= CHUNKS)
        def _():
            raw_anti(k + AHEAD - CHUNKS).start()

        cols = columns(k)
        pieces = (times - time_dev) // 64

        def rows_of(i):
            return pl.ds(pl.multiple_of(lax.rem((anti + 1) * time_dev + i * 64, times), 64), 64)

        def add(i, total):
            block = buf[rows_of(i), cols].astype(F32)
            return total + jnp.sum(block.reshape(8, 8, width), axis=0)

        total = lax.fori_loop(0, pieces, add, jnp.zeros((8, width), F32))
        mean = (jnp.sum(total, axis=0, keepdims=True) + asum_in[:, cols]) / times
        means[:, cols] = mean
        root = root_of(k)

        def weigh(i, c):
            rows = rows_of(i)
            buf[rows, cols] = (root * (buf[rows, cols].astype(F32) - mean)).astype(BF16)
            return c
        lax.fori_loop(0, pieces, weigh, 0)

        def gram(i, c):
            tile = pl.ds(pl.multiple_of(i * 256, 256), 256)
            acc[:, tile] += nt_dot(buf[:, cols], buf[tile, cols])
            return c
        lax.fori_loop(0, times // 256, gram, 0)
        mpart[:, cols] = jnp.dot(evt[...], buf[:, cols], preferred_element_type=F32)
        return carry

    def late_chunk(k, carry):
        raw_anti(k).wait_recv()
        raw_anti(k).wait_send()

        @pl.when(k + AHEAD < CHUNKS)
        def _():
            raw_anti(k + AHEAD).start()

        cols = columns(k)
        weighted = (root_of(k) * (abuf[:, cols].astype(F32) - means[:, cols])).astype(BF16)
        buf[block_rows(anti), cols] = weighted
        late[...] += nt_dot(buf[:, cols], weighted)
        proj = mpart[:, cols] + jnp.dot(
            evt[:, block_rows(anti)], weighted, preferred_element_type=F32)
        proj = (proj * inv[...]).astype(BF16)
        for p in range(8):
            msend[p, :, cols] = proj[p * 8:p * 8 + 8, :]
        return carry

    def unit(ref, g, dx, which):
        at = ((g * 4 + lax.rem(x + dx, 4)) * 2 + which) * 8
        rows = ref[pl.ds(pl.multiple_of(at, 8), 8), :]
        return jnp.concatenate([rows[:, :half], rows[:, half:]], axis=0)

    def narrow(g, dx, which):
        at = ((g * 4 + lax.rem(x + dx, 4)) * 2 + which) * 8
        return late[pl.ds(pl.multiple_of(at, 8), 8), :]

    def core_copy(dx):
        return rcopy(csend.at[dx], crecv.at[dx], c_send.at[dx], c_recv.at[dx], other)

    def x_copy(dx, sign):
        return rcopy(xsend.at[dx - 1], xrecv.at[dx - 1], x_send.at[dx - 1], x_recv.at[dx - 1],
                     (tm, sp_x(dx, sign)))

    lax.fori_loop(0, CHUNKS, early_chunk, 0)

    order = (2, 1, 3, 0)
    for dx in order:
        def pack(g, c, dx=dx):
            csend[dx, g] = unit(acc, g, dx, 1 - core).astype(BF16)
            return c
        lax.fori_loop(0, 16, pack, 0)
        core_copy(dx).start()

    lax.fori_loop(0, 1, late_chunk, 0)

    for dx in order:
        core_copy(dx).wait_recv()

        def merge(g, c, dx=dx):
            value = unit(acc, g, dx, core) + crecv[dx, g].astype(F32)
            if dx:
                xsend[dx - 1, g] = value.astype(BF16)
            else:
                part[g] = value
            return c
        lax.fori_loop(0, 16, merge, 0)
        if dx:
            x_copy(dx, 1).start()

    lax.fori_loop(1, 7, late_chunk, 0)

    for dx in (1, 2, 3):
        x_copy(dx, -1).wait_recv()

    outer = (tm_of(4, 1), (1 - y_hi) * 8 + x * 2 + core)
    inner = (tm_of(4, 1), sp)
    o_copy = rcopy(osend, orecv, o_send.at[0], o_recv.at[0], outer)
    i_copy = rcopy(isend, irecv, o_send.at[1], o_recv.at[1], inner)

    def x_total(g):
        value = part[g]
        for d in range(3):
            value = value + xrecv[d, g].astype(F32)
        return value

    def merge_x(t, c):
        osend[t] = x_total(t * 2 + 1 - y_hi).astype(BF16)
        return c
    lax.fori_loop(0, 8, merge_x, 0)
    o_copy.start()

    def merge_own(t, c):
        opart[t] = x_total(t * 2 + y_hi)
        return c
    lax.fori_loop(0, 8, merge_own, 0)

    lax.fori_loop(7, 8, late_chunk, 0)

    o_copy.wait_recv()

    def merge_o(t, c):
        other_t = (1 - y_lo) * 4 + t
        isend[t] = (opart[other_t] + orecv[other_t].astype(F32)).astype(BF16)
        return c
    lax.fori_loop(0, 4, merge_o, 0)
    i_copy.start()

    lax.fori_loop(8, 10, late_chunk, 0)

    i_copy.wait_recv()

    def y_total(t):
        own_t = y_lo * 4 + t
        return opart[own_t] + orecv[own_t].astype(F32) + irecv[t].astype(F32)

    def merge_i(t, c):
        zsend[t] = y_total(t).astype(BF16)
        return c
    lax.fori_loop(0, 4, merge_i, 0)

    def z_copy(dz, sign):
        peer = tm_of(dz, sign)
        return rcopy(zsend.at[lax.rem(peer, 4)], zrecv.at[dz - 1], z_send.at[dz - 1], z_recv.at[dz - 1],
                     (peer, sp))
    for dz in (1, 2, 3):
        z_copy(dz, 1).start()
    final_early = y_total(z)
    final[:, :half] = final_early[:8, :]
    final[:, half:] = final_early[8:, :]

    lax.fori_loop(10, CHUNKS, late_chunk, 0)

    def modes_copy(j, sign):
        peer = tm_of(j, sign)
        col = tm if sign > 0 else peer
        return rcopy(msend.at[peer], modes_out.at[:, pl.ds(pl.multiple_of(col * sub, 128), sub)],
                     m_send.at[j - 1], m_recv.at[j - 1], (peer, sp))

    lt_core = rcopy(ltc, ltc_in, lc_send.at[0], lc_recv.at[0], other)
    lr_core = rcopy(lrc, lrc_in, lc_send.at[1], lc_recv.at[1], other)

    def lt_x(dx, sign):
        return rcopy(ltx.at[dx - 1], ltx_in.at[dx - 1], lx_send.at[0, dx - 1], lx_recv.at[0, dx - 1],
                     (tm, sp_x(dx, sign)))

    def lr_x(dx, sign):
        return rcopy(lrx.at[dx - 1], lrx_in.at[dx - 1], lx_send.at[1, dx - 1], lx_recv.at[1, dx - 1],
                     (tm, sp_x(dx, sign)))

    def lt_pack(g, c):
        for dx in range(4):
            ltc[dx, g] = narrow(g, dx, 1 - core).astype(BF16)
        return c
    lax.fori_loop(0, 16, lt_pack, 0)
    lt_core.start()
    for j in range(1, 8):
        modes_copy(j, 1).start()
    modes_own = pltpu.make_async_copy(
        msend.at[tm], modes_out.at[:, pl.ds(pl.multiple_of(tm * sub, 128), sub)], m_own)
    modes_own.start()

    def turn(i, c):
        t = lax.rem(anti + 1 + i, 8)
        lrow[:, block_rows(t)] = jnp.transpose(late[block_rows(t), :])
        return c
    lax.fori_loop(0, 7, turn, 0)
    lrow[:, block_rows(anti)] = jnp.zeros((time_dev, time_dev), F32)
    for dx in range(4):
        for h in range(2):
            lrc[dx, h] = unit(lrow, h, dx, 1 - core).astype(BF16)
    lr_core.start()

    lt_core.wait_recv()
    for dx in order:
        def lt_merge(g, c, dx=dx):
            value = narrow(g, dx, core) + ltc_in[dx, g].astype(F32)
            if dx:
                ltx[dx - 1, g] = value.astype(BF16)
            else:
                lt_part[g] = value
            return c
        lax.fori_loop(0, 16, lt_merge, 0)
        if dx:
            lt_x(dx, 1).start()
    lr_core.wait_recv()
    for dx in order:
        for h in range(2):
            value = unit(lrow, h, dx, core) + lrc_in[dx, h].astype(F32)
            if dx:
                lrx[dx - 1, h] = value.astype(BF16)
            else:
                lr_part[h] = value
        if dx:
            lr_x(dx, 1).start()
    for dx in (1, 2, 3):
        lt_x(dx, -1).wait_recv()

    def lt_sum(g, c):
        value = lt_part[g]
        for d in range(3):
            value = value + ltx_in[d, g].astype(F32)
        lt_part[g] = value
        lty[g] = value.astype(BF16)
        return c
    lax.fori_loop(0, 16, lt_sum, 0)

    def lt_y(j, sign):
        t, h = yz_of(j, sign)
        return rcopy(lty.at[t * 2 + h], lty_in.at[j - 1], ly_send.at[j - 1], ly_recv.at[j - 1],
                     (t, h * 8 + x * 2 + core))

    for j in range(1, 16):
        lt_y(j, 1).start()

    for dx in (1, 2, 3):
        lr_x(dx, -1).wait_recv()
    for h in range(2):
        value = lr_part[h]
        for d in range(3):
            value = value + lrx_in[d, h].astype(F32)
        lry[h] = value.astype(BF16)

    def lr_y(i, sign):
        t, h = yz_of(LAST + 8 * i, sign)
        return rcopy(lry.at[h], lry_in.at[i], lry_send.at[i], lry_recv.at[i],
                     (t, h * 8 + x * 2 + core))

    for i in range(2):
        lr_y(i, 1).start()

    for dz in (1, 2, 3):
        z_copy(dz, -1).wait_recv()
        value = zrecv[dz - 1].astype(F32)
        final[:, :half] += value[:8, :]
        final[:, half:] += value[8:, :]
    final[:, block_rows(anti)] += lt_part[tm * 2 + y_hi]
    for j in range(1, 16):
        lt_y(j, -1).wait_recv()
        facing = (j // 4 + 1) % 2 * 4 + (j + 2) % 4
        final[:, block_rows(tm_of(facing, -1))] += lty_in[j - 1].astype(F32)
    total = jnp.concatenate([final[:, :half], final[:, half:]], axis=0)
    for i in range(2):
        lr_y(i, -1).wait_recv()
        total = total + lry_in[i].astype(F32)
    total = total / cells
    gram_out[:, :half] = total[:8, :]
    gram_out[:, half:] = total[8:, :]

    modes_own.wait()
    sum_copy.wait_send()
    for j in range(1, 8):
        modes_copy(j, -1).wait_recv()
        modes_copy(j, 1).wait_send()
    for dx in range(4):
        core_copy(dx).wait_send()
    lt_core.wait_send()
    lr_core.wait_send()
    o_copy.wait_send()
    i_copy.wait_send()
    for dx in (1, 2, 3):
        x_copy(dx, 1).wait_send()
        z_copy(dx, 1).wait_send()
        lt_x(dx, 1).wait_send()
        lr_x(dx, 1).wait_send()
    for j in range(1, 16):
        lt_y(j, 1).wait_send()
    for i in range(2):
        lr_y(i, 1).wait_send()


def hand_over(gram, modes, gram_out, modes_out, sems):
    copies = [pltpu.make_async_copy(gram, gram_out, sems.at[0]),
              pltpu.make_async_copy(modes, modes_out, sems.at[1])]
    for copy in copies:
        copy.start()
    for copy in copies:
        copy.wait()


def local(snapshots, area_weight, eigvecs, eigvals):
    tm_count = lax.axis_size("tm")
    time_dev, cell_dev = snapshots.shape
    times = time_dev * tm_count
    sub = cell_dev // tm_count
    modes_n = eigvecs.shape[1]
    half = times // 2
    vmem = pl.BlockSpec(memory_space=pltpu.VMEM)
    hbm = pl.BlockSpec(memory_space=pltpu.HBM)
    dma = pltpu.SemaphoreType.DMA
    results = pl.pallas_call(
        kernel,
        out_shape=(jax.ShapeDtypeStruct((8, times), F32), jax.ShapeDtypeStruct((8, cell_dev), BF16)),
        in_specs=[hbm] * 4,
        out_specs=(vmem, hbm),
        scratch_shapes=[
            pltpu.VMEM((times, sub), BF16),
            pltpu.VMEM((time_dev, sub), BF16),
            pltpu.VMEM((time_dev, sub), BF16),
            pltpu.VMEM((1, sub), F32),
            pltpu.VMEM((1, sub), F32),
            pltpu.VMEM((1, sub), F32),
            pltpu.VMEM((times, times), F32),
            pltpu.VMEM((times, time_dev), F32),
            pltpu.VMEM((time_dev, times), F32),
            pltpu.VMEM((modes_n, times), BF16),
            pltpu.VMEM((1, modes_n), F32),
            pltpu.VMEM((modes_n, 1), F32),
            pltpu.VMEM((sub // 128, 128), F32),
            pltpu.VMEM((modes_n, sub), F32),
            pltpu.VMEM((tm_count, 8, sub), BF16),
            pltpu.VMEM((4, 16, 16, half), BF16),
            pltpu.VMEM((4, 16, 16, half), BF16),
            pltpu.VMEM((3, 16, 16, half), BF16),
            pltpu.VMEM((3, 16, 16, half), BF16),
            pltpu.VMEM((16, 16, half), F32),
            pltpu.VMEM((8, 16, half), BF16),
            pltpu.VMEM((8, 16, half), BF16),
            pltpu.VMEM((8, 16, half), F32),
            pltpu.VMEM((4, 16, half), BF16),
            pltpu.VMEM((4, 16, half), BF16),
            pltpu.VMEM((4, 16, half), BF16),
            pltpu.VMEM((3, 16, half), BF16),
            pltpu.VMEM((4, 16, 8, 128), BF16),
            pltpu.VMEM((4, 16, 8, 128), BF16),
            pltpu.VMEM((4, 2, 16, half), BF16),
            pltpu.VMEM((4, 2, 16, half), BF16),
            pltpu.VMEM((3, 16, 8, 128), BF16),
            pltpu.VMEM((3, 16, 8, 128), BF16),
            pltpu.VMEM((3, 2, 16, half), BF16),
            pltpu.VMEM((3, 2, 16, half), BF16),
            pltpu.VMEM((16, 8, 128), F32),
            pltpu.VMEM((2, 16, half), F32),
            pltpu.VMEM((16, 8, 128), BF16),
            pltpu.VMEM((15, 8, 128), BF16),
            pltpu.VMEM((2, 16, half), BF16),
            pltpu.VMEM((2, 16, half), BF16),
            pltpu.VMEM((8, times), F32),
            dma((CHUNKS, len(FIRST))), dma((CHUNKS, len(FIRST))), dma((CHUNKS,)), dma((CHUNKS,)),
            dma, dma, dma((5,)), dma((7,)), dma((7,)), dma,
            dma((4,)), dma((4,)), dma((3,)), dma((3,)), dma((2,)), dma((2,)), dma((3,)), dma((3,)),
            dma((2,)), dma((2,)), dma((2, 3)), dma((2, 3)),
            dma((15,)), dma((15,)), dma((2,)), dma((2,)),
        ],
        compiler_params=pltpu.CompilerParams(
            collective_id=0, has_side_effects=True, vmem_limit_bytes=48 << 20),
        cost_estimate=pl.CostEstimate(
            flops=2 * times * times * sub, bytes_accessed=2 * times * sub, transcendentals=0),
    )(*[pltpu.with_memory_space_constraint(v, pltpu.HBM) for v in (
        snapshots, area_weight.reshape(-1, 128), eigvecs.T, eigvals.reshape(1, -1))])
    return pl.pallas_call(
        hand_over,
        out_shape=[jax.ShapeDtypeStruct(v.shape, v.dtype) for v in results],
        in_specs=[vmem] * 2,
        out_specs=[pl.BlockSpec(memory_space=pltpu.HBM)] * 2,
        scratch_shapes=[dma((2,))],
        compiler_params=pltpu.CompilerParams(vmem_limit_bytes=2 << 20),
    )(*results)


def solution(mesh):
    in_specs = (P("tm", "space"), P("space"), P(), P())
    out_specs = (P(("tm", "space"), None), P("tm", "space"))
    return jax.shard_map(local, mesh=mesh, in_specs=in_specs, out_specs=out_specs, check_vma=False)
```

```python
import jax
import jax.numpy as jnp
from jax import lax
from jax.experimental import pallas as pl
from jax.experimental.pallas import tpu as pltpu
from jax.sharding import PartitionSpec as P

MESH = pl.DeviceIdType.MESH
CHUNKS = 12
AHEAD = 6
FIRST = (1, 2, 3, 4, 5, 7)
LAST = 6
BF16, F32 = jnp.bfloat16, jnp.float32


def kernel(snap, area, evt_in, evals_in, gram_out, modes_out,
           buf, abuf, sbuf, asum, asum_in, means, acc, late, lrow, evt, evals, inv, area_v, mpart, msend,
           csend, crecv, xsend, xrecv, part, osend, orecv, opart, isend, irecv, zsend, zrecv,
           ltc, ltc_in, lrc, lrc_in, ltx, ltx_in, lrx, lrx_in,
           lt_part, lr_part, lty, lty_in, lry, lry_in, final,
           s_send, s_recv, a_send, a_recv, t_send, t_recv, s_local, m_send, m_recv, m_own,
           c_send, c_recv, x_send, x_recv, o_send, o_recv, z_send, z_recv, lc_send, lc_recv, lx_send, lx_recv,
           ly_send, ly_recv, lry_send, lry_recv):
    time_dev, cell_dev = snap.shape
    times, sub = buf.shape
    width = sub // CHUNKS
    modes_n = evt.shape[0]
    cells = cell_dev * 16
    half = times // 2

    tm = lax.axis_index("tm")
    sp = lax.axis_index("space")
    y_lo, z = tm // 4, lax.rem(tm, 4)
    y_hi, x, core = sp // 8, lax.rem(sp // 2, 4), lax.rem(sp, 2)

    def tm_of(j, sign):
        return lax.rem(y_lo + j // 4, 2) * 4 + lax.rem(z + sign * (j % 4) + 4, 4)

    def sp_x(dx, sign):
        return y_hi * 8 + lax.rem(x + sign * dx + 4, 4) * 2 + core

    def yz_of(j, sign):
        return tm_of(j % 8, sign), lax.rem(y_hi + j // 8, 2)

    def yz_dev(j, sign):
        t, h = yz_of(j, sign)
        return (t, h * 8 + x * 2 + core)

    def rcopy(src, dst, send, recv, device):
        return pltpu.make_async_remote_copy(
            src_ref=src, dst_ref=dst, send_sem=send, recv_sem=recv,
            device_id=device, device_id_type=MESH)

    other = (tm, sp + 1 - 2 * core)
    anti = tm_of(LAST, 1)

    barrier = pltpu.get_barrier_semaphore()
    partners = [yz_dev(j, 1) for j in range(1, 16)] + [other] + [(tm, sp_x(d, 1)) for d in (1, 2, 3)]
    for device in partners:
        pl.semaphore_signal(barrier, inc=1, device_id=device, device_id_type=MESH)
    pl.semaphore_wait(barrier, len(partners))

    def columns(k):
        return pl.ds(pl.multiple_of(k * width, 128), width)

    def block_rows(t):
        return pl.ds(pl.multiple_of(t * time_dev, 128), time_dev)

    def raw(k, i, sign):
        peer = tm_of(FIRST[i], sign)
        row = tm if sign > 0 else peer
        return rcopy(snap.at[:, pl.ds(pl.multiple_of(peer * sub + k * width, 128), width)],
                     buf.at[block_rows(row), columns(k)],
                     s_send.at[k, i], s_recv.at[k, i], (peer, sp))

    def raw_anti(k):
        return rcopy(snap.at[:, pl.ds(pl.multiple_of(anti * sub + k * width, 128), width)],
                     abuf.at[:, columns(k)], a_send.at[k], a_recv.at[k], (anti, sp))

    def start_chunk(k):
        for i in range(len(FIRST)):
            raw(k, i, 1).start()

    area_rows = sub // 128
    local_copies = [pltpu.make_async_copy(src, dst, s_local.at[i]) for i, (src, dst) in enumerate((
        (snap.at[:, pl.ds(pl.multiple_of(anti * sub, 128), sub)], sbuf),
        (snap.at[:, pl.ds(pl.multiple_of(tm * sub, 128), sub)], buf.at[block_rows(tm), :]),
        (area.at[pl.ds(pl.multiple_of(tm * area_rows, 8), area_rows), :], area_v),
        (evals_in, evals),
        (evt_in, evt),
    ))]
    start_chunk(0)
    for copy in local_copies:
        copy.start()

    local_copies[0].wait()

    def share(k, c):
        asum[:, columns(k)] = jnp.sum(sbuf[:, columns(k)].astype(F32), axis=0, keepdims=True)
        return c
    lax.fori_loop(0, CHUNKS, share, 0)
    sum_copy = rcopy(asum, asum_in, t_send, t_recv, (anti, sp))
    sum_copy.start()
    for k in range(1, AHEAD):
        start_chunk(k)

    acc[...] = jnp.zeros_like(acc)
    late[...] = jnp.zeros_like(late)

    def clear(i, c):
        buf[pl.ds(pl.multiple_of(anti * time_dev + i * 16, 16), 16), :] = jnp.zeros((16, sub), BF16)
        return c
    lax.fori_loop(0, time_dev // 16, clear, 0)
    for copy in local_copies[1:]:
        copy.wait()
    eye = lax.broadcasted_iota(jnp.int32, (modes_n, modes_n), 0) == lax.broadcasted_iota(
        jnp.int32, (modes_n, modes_n), 1)
    inv[...] = 1.0 / jnp.sqrt(jnp.sum(
        jnp.where(eye, jnp.broadcast_to(evals[...], (modes_n, modes_n)), 0.0), axis=1, keepdims=True))
    area_v[...] = jnp.sqrt(area_v[...])
    sum_copy.wait_recv()

    strips = width // 128

    def root_of(k):
        return jnp.concatenate([area_v[pl.ds(k * strips + s, 1), :] for s in range(strips)], axis=1)

    def nt_dot(a, b):
        return lax.dot_general(a, b, (((1,), (1,)), ((), ())), preferred_element_type=F32)

    def early_chunk(k, carry):
        for i in range(len(FIRST)):
            raw(k, i, -1).wait_recv()
        for i in range(len(FIRST)):
            raw(k, i, 1).wait_send()

        @pl.when(k + AHEAD < CHUNKS)
        def _():
            start_chunk(k + AHEAD)

        @pl.when(k + AHEAD >= CHUNKS)
        def _():
            raw_anti(k + AHEAD - CHUNKS).start()

        cols = columns(k)
        pieces = (times - time_dev) // 64

        def rows_of(i):
            return pl.ds(pl.multiple_of(lax.rem((anti + 1) * time_dev + i * 64, times), 64), 64)

        def add(i, total):
            block = buf[rows_of(i), cols].astype(F32)
            return total + jnp.sum(block.reshape(8, 8, width), axis=0)

        total = lax.fori_loop(0, pieces, add, jnp.zeros((8, width), F32))
        mean = (jnp.sum(total, axis=0, keepdims=True) + asum_in[:, cols]) / times
        means[:, cols] = mean
        root = root_of(k)

        def weigh(i, c):
            rows = rows_of(i)
            buf[rows, cols] = (root * (buf[rows, cols].astype(F32) - mean)).astype(BF16)
            return c
        lax.fori_loop(0, pieces, weigh, 0)

        def gram(i, c):
            tile = pl.ds(pl.multiple_of(i * 256, 256), 256)
            acc[:, tile] += nt_dot(buf[:, cols], buf[tile, cols])
            return c
        lax.fori_loop(0, times // 256, gram, 0)
        mpart[:, cols] = jnp.dot(evt[...], buf[:, cols], preferred_element_type=F32)
        return carry

    def late_chunk(k, carry):
        raw_anti(k).wait_recv()
        raw_anti(k).wait_send()

        @pl.when(k + AHEAD < CHUNKS)
        def _():
            raw_anti(k + AHEAD).start()

        cols = columns(k)
        weighted = (root_of(k) * (abuf[:, cols].astype(F32) - means[:, cols])).astype(BF16)
        buf[block_rows(anti), cols] = weighted
        late[...] += nt_dot(buf[:, cols], weighted)
        proj = mpart[:, cols] + jnp.dot(
            evt[:, block_rows(anti)], weighted, preferred_element_type=F32)
        proj = (proj * inv[...]).astype(BF16)
        for p in range(8):
            msend[p, :, cols] = proj[p * 8:p * 8 + 8, :]
        return carry

    def unit(ref, g, dx, which):
        at = ((g * 4 + lax.rem(x + dx, 4)) * 2 + which) * 8
        rows = ref[pl.ds(pl.multiple_of(at, 8), 8), :]
        return jnp.concatenate([rows[:, :half], rows[:, half:]], axis=0)

    def narrow(g, dx, which):
        at = ((g * 4 + lax.rem(x + dx, 4)) * 2 + which) * 8
        return late[pl.ds(pl.multiple_of(at, 8), 8), :]

    def core_copy(dx):
        return rcopy(csend.at[dx], crecv.at[dx], c_send.at[dx], c_recv.at[dx], other)

    def x_copy(dx, sign):
        return rcopy(xsend.at[dx - 1], xrecv.at[dx - 1], x_send.at[dx - 1], x_recv.at[dx - 1],
                     (tm, sp_x(dx, sign)))

    lax.fori_loop(0, CHUNKS, early_chunk, 0)

    order = (2, 1, 3, 0)
    for dx in order:
        def pack(g, c, dx=dx):
            csend[dx, g] = unit(acc, g, dx, 1 - core).astype(BF16)
            return c
        lax.fori_loop(0, 16, pack, 0)
        core_copy(dx).start()

    lax.fori_loop(0, 1, late_chunk, 0)

    for dx in order:
        core_copy(dx).wait_recv()

        def merge(g, c, dx=dx):
            value = unit(acc, g, dx, core) + crecv[dx, g].astype(F32)
            if dx:
                xsend[dx - 1, g] = value.astype(BF16)
            else:
                part[g] = value
            return c
        lax.fori_loop(0, 16, merge, 0)
        if dx:
            x_copy(dx, 1).start()

    lax.fori_loop(1, 7, late_chunk, 0)

    for dx in (1, 2, 3):
        x_copy(dx, -1).wait_recv()

    outer = (tm_of(4, 1), (1 - y_hi) * 8 + x * 2 + core)
    inner = (tm_of(4, 1), sp)
    o_copy = rcopy(osend, orecv, o_send.at[0], o_recv.at[0], outer)
    i_copy = rcopy(isend, irecv, o_send.at[1], o_recv.at[1], inner)

    def x_total(g):
        value = part[g]
        for d in range(3):
            value = value + xrecv[d, g].astype(F32)
        return value

    def merge_x(t, c):
        osend[t] = x_total(t * 2 + 1 - y_hi).astype(BF16)
        return c
    lax.fori_loop(0, 8, merge_x, 0)
    o_copy.start()

    def merge_own(t, c):
        opart[t] = x_total(t * 2 + y_hi)
        return c
    lax.fori_loop(0, 8, merge_own, 0)

    lax.fori_loop(7, 8, late_chunk, 0)

    o_copy.wait_recv()

    def merge_o(t, c):
        other_t = (1 - y_lo) * 4 + t
        isend[t] = (opart[other_t] + orecv[other_t].astype(F32)).astype(BF16)
        return c
    lax.fori_loop(0, 4, merge_o, 0)
    i_copy.start()

    lax.fori_loop(8, CHUNKS, late_chunk, 0)

    def modes_copy(j, sign):
        peer = tm_of(j, sign)
        col = tm if sign > 0 else peer
        return rcopy(msend.at[peer], modes_out.at[:, pl.ds(pl.multiple_of(col * sub, 128), sub)],
                     m_send.at[j - 1], m_recv.at[j - 1], (peer, sp))

    lt_core = rcopy(ltc, ltc_in, lc_send.at[0], lc_recv.at[0], other)
    lr_core = rcopy(lrc, lrc_in, lc_send.at[1], lc_recv.at[1], other)

    def lt_x(dx, sign):
        return rcopy(ltx.at[dx - 1], ltx_in.at[dx - 1], lx_send.at[0, dx - 1], lx_recv.at[0, dx - 1],
                     (tm, sp_x(dx, sign)))

    def lr_x(dx, sign):
        return rcopy(lrx.at[dx - 1], lrx_in.at[dx - 1], lx_send.at[1, dx - 1], lx_recv.at[1, dx - 1],
                     (tm, sp_x(dx, sign)))

    def lt_pack(g, c):
        for dx in range(4):
            ltc[dx, g] = narrow(g, dx, 1 - core).astype(BF16)
        return c
    lax.fori_loop(0, 16, lt_pack, 0)
    lt_core.start()
    for j in range(1, 8):
        modes_copy(j, 1).start()
    modes_own = pltpu.make_async_copy(
        msend.at[tm], modes_out.at[:, pl.ds(pl.multiple_of(tm * sub, 128), sub)], m_own)
    modes_own.start()

    def turn(i, c):
        t = lax.rem(anti + 1 + i, 8)
        lrow[:, block_rows(t)] = jnp.transpose(late[block_rows(t), :])
        return c
    lax.fori_loop(0, 7, turn, 0)
    lrow[:, block_rows(anti)] = jnp.zeros((time_dev, time_dev), F32)
    for dx in range(4):
        for h in range(2):
            lrc[dx, h] = unit(lrow, h, dx, 1 - core).astype(BF16)
    lr_core.start()

    lt_core.wait_recv()
    for dx in order:
        def lt_merge(g, c, dx=dx):
            value = narrow(g, dx, core) + ltc_in[dx, g].astype(F32)
            if dx:
                ltx[dx - 1, g] = value.astype(BF16)
            else:
                lt_part[g] = value
            return c
        lax.fori_loop(0, 16, lt_merge, 0)
        if dx:
            lt_x(dx, 1).start()
    lr_core.wait_recv()
    for dx in order:
        for h in range(2):
            value = unit(lrow, h, dx, core) + lrc_in[dx, h].astype(F32)
            if dx:
                lrx[dx - 1, h] = value.astype(BF16)
            else:
                lr_part[h] = value
        if dx:
            lr_x(dx, 1).start()
    i_copy.wait_recv()

    def y_total(t):
        own_t = y_lo * 4 + t
        return opart[own_t] + orecv[own_t].astype(F32) + irecv[t].astype(F32)

    def merge_i(t, c):
        zsend[t] = y_total(t).astype(BF16)
        return c
    lax.fori_loop(0, 4, merge_i, 0)

    def z_copy(dz, sign):
        peer = tm_of(dz, sign)
        return rcopy(zsend.at[lax.rem(peer, 4)], zrecv.at[dz - 1], z_send.at[dz - 1], z_recv.at[dz - 1],
                     (peer, sp))
    for dz in (1, 2, 3):
        z_copy(dz, 1).start()
    final_early = y_total(z)
    final[:, :half] = final_early[:8, :]
    final[:, half:] = final_early[8:, :]

    for dx in (1, 2, 3):
        lt_x(dx, -1).wait_recv()

    def lt_sum(g, c):
        value = lt_part[g]
        for d in range(3):
            value = value + ltx_in[d, g].astype(F32)
        lt_part[g] = value
        lty[g] = value.astype(BF16)
        return c
    lax.fori_loop(0, 16, lt_sum, 0)

    def lt_y(j, sign):
        t, h = yz_of(j, sign)
        return rcopy(lty.at[t * 2 + h], lty_in.at[j - 1], ly_send, ly_recv,
                     (t, h * 8 + x * 2 + core))

    for j in range(1, 16):
        lt_y(j, 1).start()

    for dx in (1, 2, 3):
        lr_x(dx, -1).wait_recv()
    for h in range(2):
        value = lr_part[h]
        for d in range(3):
            value = value + lrx_in[d, h].astype(F32)
        lry[h] = value.astype(BF16)

    def lr_y(i, sign):
        t, h = yz_of(LAST + 8 * i, sign)
        return rcopy(lry.at[h], lry_in.at[i], lry_send.at[i], lry_recv.at[i],
                     (t, h * 8 + x * 2 + core))

    for i in range(2):
        lr_y(i, 1).start()

    for dz in (1, 2, 3):
        z_copy(dz, -1).wait_recv()
        value = zrecv[dz - 1].astype(F32)
        final[:, :half] += value[:8, :]
        final[:, half:] += value[8:, :]
    final[:, block_rows(anti)] += lt_part[tm * 2 + y_hi]
    all_y = rcopy(lty.at[pl.ds(0, 15)], lty_in, ly_send, ly_recv, other)
    all_y.wait_recv()
    for j in range(1, 16):
        facing = (j // 4 + 1) % 2 * 4 + (j + 2) % 4
        final[:, block_rows(tm_of(facing, -1))] += lty_in[j - 1].astype(F32)
    total = jnp.concatenate([final[:, :half], final[:, half:]], axis=0)
    for i in range(2):
        lr_y(i, -1).wait_recv()
        total = total + lry_in[i].astype(F32)
    total = total / cells
    gram_out[:, :half] = total[:8, :]
    gram_out[:, half:] = total[8:, :]

    modes_own.wait()
    sum_copy.wait_send()
    for j in range(1, 8):
        modes_copy(j, -1).wait_recv()
        modes_copy(j, 1).wait_send()
    for dx in range(4):
        core_copy(dx).wait_send()
    lt_core.wait_send()
    lr_core.wait_send()
    o_copy.wait_send()
    i_copy.wait_send()
    for dx in (1, 2, 3):
        x_copy(dx, 1).wait_send()
        z_copy(dx, 1).wait_send()
        lt_x(dx, 1).wait_send()
        lr_x(dx, 1).wait_send()
    all_y.wait_send()
    for i in range(2):
        lr_y(i, 1).wait_send()


def hand_over(gram, modes, gram_out, modes_out, sems):
    copies = [pltpu.make_async_copy(gram, gram_out, sems.at[0]),
              pltpu.make_async_copy(modes, modes_out, sems.at[1])]
    for copy in copies:
        copy.start()
    for copy in copies:
        copy.wait()


def local(snapshots, area_weight, eigvecs, eigvals):
    tm_count = lax.axis_size("tm")
    time_dev, cell_dev = snapshots.shape
    times = time_dev * tm_count
    sub = cell_dev // tm_count
    modes_n = eigvecs.shape[1]
    half = times // 2
    vmem = pl.BlockSpec(memory_space=pltpu.VMEM)
    hbm = pl.BlockSpec(memory_space=pltpu.HBM)
    dma = pltpu.SemaphoreType.DMA
    results = pl.pallas_call(
        kernel,
        out_shape=(jax.ShapeDtypeStruct((8, times), F32), jax.ShapeDtypeStruct((8, cell_dev), BF16)),
        in_specs=[hbm] * 4,
        out_specs=(vmem, hbm),
        scratch_shapes=[
            pltpu.VMEM((times, sub), BF16),
            pltpu.VMEM((time_dev, sub), BF16),
            pltpu.VMEM((time_dev, sub), BF16),
            pltpu.VMEM((1, sub), F32),
            pltpu.VMEM((1, sub), F32),
            pltpu.VMEM((1, sub), F32),
            pltpu.VMEM((times, times), F32),
            pltpu.VMEM((times, time_dev), F32),
            pltpu.VMEM((time_dev, times), F32),
            pltpu.VMEM((modes_n, times), BF16),
            pltpu.VMEM((1, modes_n), F32),
            pltpu.VMEM((modes_n, 1), F32),
            pltpu.VMEM((sub // 128, 128), F32),
            pltpu.VMEM((modes_n, sub), F32),
            pltpu.VMEM((tm_count, 8, sub), BF16),
            pltpu.VMEM((4, 16, 16, half), BF16),
            pltpu.VMEM((4, 16, 16, half), BF16),
            pltpu.VMEM((3, 16, 16, half), BF16),
            pltpu.VMEM((3, 16, 16, half), BF16),
            pltpu.VMEM((16, 16, half), F32),
            pltpu.VMEM((8, 16, half), BF16),
            pltpu.VMEM((8, 16, half), BF16),
            pltpu.VMEM((8, 16, half), F32),
            pltpu.VMEM((4, 16, half), BF16),
            pltpu.VMEM((4, 16, half), BF16),
            pltpu.VMEM((4, 16, half), BF16),
            pltpu.VMEM((3, 16, half), BF16),
            pltpu.VMEM((4, 16, 8, 128), BF16),
            pltpu.VMEM((4, 16, 8, 128), BF16),
            pltpu.VMEM((4, 2, 16, half), BF16),
            pltpu.VMEM((4, 2, 16, half), BF16),
            pltpu.VMEM((3, 16, 8, 128), BF16),
            pltpu.VMEM((3, 16, 8, 128), BF16),
            pltpu.VMEM((3, 2, 16, half), BF16),
            pltpu.VMEM((3, 2, 16, half), BF16),
            pltpu.VMEM((16, 8, 128), F32),
            pltpu.VMEM((2, 16, half), F32),
            pltpu.VMEM((16, 8, 128), BF16),
            pltpu.VMEM((15, 8, 128), BF16),
            pltpu.VMEM((2, 16, half), BF16),
            pltpu.VMEM((2, 16, half), BF16),
            pltpu.VMEM((8, times), F32),
            dma((CHUNKS, len(FIRST))), dma((CHUNKS, len(FIRST))), dma((CHUNKS,)), dma((CHUNKS,)),
            dma, dma, dma((5,)), dma((7,)), dma((7,)), dma,
            dma((4,)), dma((4,)), dma((3,)), dma((3,)), dma((2,)), dma((2,)), dma((3,)), dma((3,)),
            dma((2,)), dma((2,)), dma((2, 3)), dma((2, 3)),
            dma, dma, dma((2,)), dma((2,)),
        ],
        compiler_params=pltpu.CompilerParams(
            collective_id=0, has_side_effects=True, vmem_limit_bytes=48 << 20),
        cost_estimate=pl.CostEstimate(
            flops=2 * times * times * sub, bytes_accessed=2 * times * sub, transcendentals=0),
    )(*[pltpu.with_memory_space_constraint(v, pltpu.HBM) for v in (
        snapshots, area_weight.reshape(-1, 128), eigvecs.T, eigvals.reshape(1, -1))])
    return pl.pallas_call(
        hand_over,
        out_shape=[jax.ShapeDtypeStruct(v.shape, v.dtype) for v in results],
        in_specs=[vmem] * 2,
        out_specs=[pl.BlockSpec(memory_space=pltpu.HBM)] * 2,
        scratch_shapes=[dma((2,))],
        compiler_params=pltpu.CompilerParams(vmem_limit_bytes=2 << 20),
    )(*results)


def solution(mesh):
    in_specs = (P("tm", "space"), P("space"), P(), P())
    out_specs = (P(("tm", "space"), None), P("tm", "space"))
    return jax.shard_map(local, mesh=mesh, in_specs=in_specs, out_specs=out_specs, check_vma=False)
```
